32 devices in a mesh: wide: 2 (over y), blk: 4 (over z), head: 4 (over x, core).
Axes of the slice: x: 2, y: 2, z: 4, core: 2. Of those that a mesh axis runs over, the one named last changes fastest.
Arguments:
- tokens: bfloat16 [8, 4, 256, 1536], P('blk', 'wide', 'head'), may hold values from -6 to 6
- positions: int32 [8, 4, 256], P('blk', 'wide', 'head'), may hold values from 0 to 2047, as said below
- block_order: int32 [8], replicated, may hold values from 0 to 7, as said below
- w_qkv: bfloat16 [1536, 2048], P('wide'), may hold values from -0.15625 to 0.15625
- qkv_bias: bfloat16 [2048], P('wide'), may hold values from -0.59765625 to 0.59765625
- w_out: bfloat16 [1536, 1536], P('wide'), may hold values from -0.875 to 0.875
- w_gate_up: bfloat16 [1536, 17920], P('wide'), may hold values from -0.15625 to 0.15625
- w_down: bfloat16 [1536, 8960], P('wide'), may hold values from -0.0625 to 0.0625
- gain_attn: bfloat16 [1536], P('wide'), may hold values from 0.25 to 1.75
- gain_mlp: bfloat16 [1536], P('wide'), may hold values from 0.25 to 1.75
- cotangent: bfloat16 [8, 4, 256, 1536], P('blk', 'wide', 'head'), may hold values from -6 to 6
Outputs:
- output: bfloat16 [8, 4, 256, 1536], P('blk', 'wide', 'head')
- input_grad: bfloat16 [8, 4, 256, 1536], P('blk', 'wide', 'head')
- qkv_grad: float32 [1536, 2048], P('wide')
- bias_grad: float32 [2048], P('wide')
- out_grad: float32 [1536, 1536], P('wide')
- gate_up_grad: float32 [1536, 17920], P('wide')
- down_grad: float32 [1536, 8960], P('wide')
- gain_attn_grad: float32 [1536], P('wide')
- gain_mlp_grad: float32 [1536], P('wide')
The draws below stay inside these ranges and needn't reach their ends.
Inputs may be any that keep to these rules, and one draw needn't show every extreme that they name: Each number from 0 to 7 stands once; slot j of every sequence holds that sequence's block number block_order[j], 256 consecutive tokens. Read in the order of block numbers, a sequence's positions count 0, 1, 2, ... from its first token and restart at 0 at the first token of each packed document; one sequence is a single document that counts to 2047.
All inputs are finite; a program needn't handle non-finite values.
Results may differ from the reference program's by a relative error of at most 0.017.
Values may be sent and summed in bfloat16 or wider, within the bound.
No kernel may reach another device: no remote copies, remote signals or barrier semaphores. Data moves between devices by JAX's collectives and lax.ppermute only.
A program may use at most 704 MiB of HBM per device.

```python
import jax
import jax.numpy as jnp
from jax import lax

D = 1536
FF = 8960
QUERY_HEADS = 12
KEY_VALUE_HEADS = 2
HEAD_SIZE = 128
SEQ_LEN = 2048
QKV = 2048
BLOCKS = 8
BROWS = 256
SEQS = 4


def shared_order(key):
    return jax.random.permutation(jax.random.fold_in(key, 17), BLOCKS).astype(jnp.int32)


def draw_block_order(key, part):
    return shared_order(key)


def draw_positions(key, part):
    slot_order = shared_order(key)
    key = jax.random.fold_in(key, 29)
    start_key, whole_key = jax.random.split(key)
    starts = jax.random.randint(start_key, (SEQS, SEQ_LEN), 0, SEQ_LEN // 4) == 0
    whole_seq = jax.random.randint(whole_key, (), 0, SEQS)
    seq_index = jnp.arange(SEQS, dtype=jnp.int32)[:, None]
    index_row = jnp.arange(SEQ_LEN, dtype=jnp.int32)[None, :]
    starts = starts & (seq_index != whole_seq) | (index_row == 0)
    begins = lax.cummax(jnp.where(starts, index_row, 0), axis=1)
    causal = (index_row - begins).reshape(SEQS, BLOCKS, BROWS)
    stored = jnp.take(causal, slot_order, axis=1)
    return jnp.transpose(stored, (1, 0, 2)).astype(jnp.int32)


def spiked(entries, own_key, source, target, shards_of, factor):
    owner, partner = [(jnp.arange(entries.shape[axis_at]) // (entries.shape[axis_at] // shards_of)).reshape([-1 if axis == axis_at else 1 for axis in range(entries.ndim)]) for axis_at in (source, target)]
    chosen = jax.random.permutation(own_key, shards_of)[partner]
    strong = (owner == chosen) | (owner == (partner + shards_of // 2) % shards_of)
    return jnp.where(strong, factor * entries, entries)


def shard_levels(own_key, shape, shards, smallest, largest):
    factor_of, own = 1.0, jax.random.fold_in(own_key, 6)
    for dim, blocks in shards:
        draws = jnp.exp(jax.random.uniform(jax.random.fold_in(own, dim), (blocks,), jnp.float32, smallest / len(shards), largest / len(shards)))
        factor_of = factor_of * jnp.repeat(draws, shape[dim] // blocks).reshape([-1 if axis == dim else 1 for axis in range(len(shape))])
    return factor_of


def gaussian(rng, extent, width, bound, cuts=(), kind=jnp.bfloat16):
    entries = jax.random.normal(rng, extent, jnp.float32) * width
    if len(cuts) > 0:
        entries = shard_levels(rng, extent, cuts, -0.22, 0.18) * entries
    return jnp.clip(entries, min=-bound, max=bound).astype(kind)


def bell_draw_with(key, dims, spread, limit, shards, heavy, kind=jnp.bfloat16):
    result = spread * jax.random.normal(key, dims, jnp.float32)
    if shards:
        result = result * shard_levels(key, dims, shards, -0.22, 0.18)
    return jnp.clip(spiked(result, jax.random.fold_in(key, 3), *heavy), -limit, limit).astype(kind)


def setup_inputs(seed: int = 0) -> dict:
    key_list = jax.random.split(jax.random.key(seed), 12)
    tokens = bell_draw_with(key_list[0], (BLOCKS, SEQS, BROWS, D), 1.0, 6.0, ((0, 4), (1, 2), (2, 4)), (1, 3, 2, 2.0))
    positions = draw_positions(jax.random.fold_in(key_list[11], 71), 0)
    block_order = draw_block_order(jax.random.fold_in(key_list[11], 71), 0)
    w_qkv = gaussian(key_list[3], (D, QKV), D ** -0.5, 0.15625, ((0, 2),))
    qkv_bias = gaussian(key_list[4], (QKV,), 0.1, 0.59765625, ((0, 2),))
    w_out = gaussian(key_list[5], (D, QUERY_HEADS * HEAD_SIZE), (QUERY_HEADS * HEAD_SIZE // 32) ** -0.5, 0.875, ((0, 2),))
    w_gate_up = gaussian(key_list[6], (D, 2 * FF), D ** -0.5, 0.15625, ((0, 2),))
    w_down = gaussian(key_list[7], (D, FF), FF ** -0.5, 0.0625, ((0, 2),))
    gain_attn = jnp.clip(1.0 + 0.15 * jax.random.normal(key_list[8], (D,), jnp.float32), 0.25, 1.75).astype(jnp.bfloat16)
    gain_mlp = jnp.clip(1.0 + 0.15 * jax.random.normal(key_list[9], (D,), jnp.float32), 0.25, 1.75).astype(jnp.bfloat16)
    cotangent = bell_draw_with(key_list[10], (BLOCKS, SEQS, BROWS, D), 1.0, 6.0, ((0, 4), (1, 2), (2, 4)), (0, 3, 4, 2.0))
    return dict(tokens=tokens, positions=positions, block_order=block_order, w_qkv=w_qkv, qkv_bias=qkv_bias, w_out=w_out, w_gate_up=w_gate_up, w_down=w_down, gain_attn=gain_attn, gain_mlp=gain_mlp, cotangent=cotangent)


norm_eps = 1e-06
rope_theta = 1000000.0
masked_score = -1e+30

@jax.custom_vjp
def lower_half(v):
    return lax.optimization_barrier(v.astype(jnp.bfloat16)).astype(jnp.float32)

@jax.custom_vjp
def low_back(v):
    return v

def low_keep(v):
    return (lower_half(v), None)

def low_pass(kept, grad):
    return (grad,)

def back_keep(v):
    return (v, None)

def back_low(kept, grad):
    return (lower_half(grad),)
lower_half.defvjp(low_keep, low_pass)
low_back.defvjp(back_keep, back_low)

def rms_norm(values, gain_row):
    inverse = lax.rsqrt(lax.optimization_barrier(jnp.mean(values * values, axis=-1, keepdims=True)) + norm_eps)
    return values * inverse * gain_row

def half_turn(values):
    half_size = values.shape[-1] // 2
    return jnp.concatenate([-values[..., half_size:], values[..., :half_size]], axis=-1)

def rotate_pairs(values, cosine_table, sine_values):
    return values * cosine_table + half_turn(values) * sine_values

def rope_tables(positions):
    frequency = rope_theta ** (-jnp.arange(0, HEAD_SIZE, 2).astype(jnp.float32) / HEAD_SIZE)
    angles = positions.astype(jnp.float32)[:, None] * frequency[None, :]
    angles = jnp.concatenate([angles, angles], axis=-1)
    return (jnp.cos(angles), jnp.sin(angles))

def attend_block(query_tile_block, key_row_set, value_row_set, first_row):
    query_group_size = QUERY_HEADS // KEY_VALUE_HEADS
    block_row_set = query_tile_block.shape[0]
    grouped_heads = query_tile_block.reshape(block_row_set, KEY_VALUE_HEADS, query_group_size, HEAD_SIZE)
    scores = jnp.einsum('qgjd,kgd->gjqk', grouped_heads, key_row_set, precision=lax.Precision.HIGHEST) * HEAD_SIZE ** (-0.5)
    scores = low_back(scores)
    query_index = first_row + jnp.arange(block_row_set, dtype=jnp.int32)
    key_index = jnp.arange(key_row_set.shape[0], dtype=jnp.int32)
    allowed = key_index[None, :] <= query_index[:, None]
    masked = jnp.where(allowed, scores, masked_score)
    top_score = lax.optimization_barrier(jnp.max(masked, axis=-1, keepdims=True))
    exponent = jnp.where(allowed, jnp.exp(masked - top_score), 0.0)
    probs = lower_half(exponent / lax.optimization_barrier(jnp.sum(exponent, axis=-1, keepdims=True)))
    mixed_rows = jnp.einsum('gjqk,kgd->qgjd', probs, value_row_set, precision=lax.Precision.HIGHEST)
    return mixed_rows.reshape(block_row_set, QUERY_HEADS * HEAD_SIZE)

def attend_sequence(bundle):
    query_rows, key_row_set, value_row_set = bundle
    block_size = min(512, SEQ_LEN)
    blocked = query_rows.reshape(SEQ_LEN // block_size, block_size, QUERY_HEADS, HEAD_SIZE)
    first_rows = jnp.arange(SEQ_LEN // block_size, dtype=jnp.int32) * block_size

    def block_step(inner_bundle):
        return attend_block(inner_bundle[0], key_row_set, value_row_set, inner_bundle[1])
    outputs = lax.map(jax.checkpoint(block_step), (blocked, first_rows))
    return outputs.reshape(SEQ_LEN, QUERY_HEADS * HEAD_SIZE)

def sequence_step(unused_carry, bundle):
    return (unused_carry, attend_sequence(bundle))

def to_causal(array, inverse_order):
    head_count = array.shape[1]
    arranged = array.reshape(BLOCKS, SEQS, BROWS, head_count, HEAD_SIZE)
    arranged = jnp.take(arranged, inverse_order, axis=0)
    return jnp.transpose(arranged, (1, 0, 2, 3, 4)).reshape(SEQS, SEQ_LEN, head_count, HEAD_SIZE)

def to_slots(array, block_order):
    features = array.shape[-1]
    arranged = array.reshape(SEQS, BLOCKS, BROWS, features)
    arranged = jnp.take(arranged, block_order, axis=1)
    return jnp.transpose(arranged, (1, 0, 2, 3)).reshape(-1, features)

def decoder_layer(tokens_f, w_qkv_f, bias_f, w_out_f, w_gate_up_f, w_down_f, gain_attn_f, gain_mlp_f, cosine_table, sine_values, block_order, inverse_order):
    highest = lax.Precision.HIGHEST
    flat_tokens = tokens_f.reshape(-1, D)
    normed_attn = lower_half(rms_norm(flat_tokens, gain_attn_f))
    projected_rows = low_back(jnp.dot(normed_attn, w_qkv_f, precision=highest) + bias_f)
    query_total_width = QUERY_HEADS * HEAD_SIZE
    key_value_width = KEY_VALUE_HEADS * HEAD_SIZE
    queries = lower_half(rotate_pairs(projected_rows[:, :query_total_width].reshape(-1, QUERY_HEADS, HEAD_SIZE), cosine_table[:, None, :], sine_values[:, None, :]))
    key_row_set = lower_half(rotate_pairs(projected_rows[:, query_total_width:query_total_width + key_value_width].reshape(-1, KEY_VALUE_HEADS, HEAD_SIZE), cosine_table[:, None, :], sine_values[:, None, :]))
    value_row_set = lower_half(projected_rows[:, query_total_width + key_value_width:].reshape(-1, KEY_VALUE_HEADS, HEAD_SIZE))
    sequences = (to_causal(queries, inverse_order), to_causal(key_row_set, inverse_order), to_causal(value_row_set, inverse_order))
    unused_carry, attention = lax.scan(jax.checkpoint(sequence_step), None, sequences)
    attended = low_back(lower_half(to_slots(attention, block_order)))
    branch = low_back(jnp.dot(attended, w_out_f.T, precision=highest))
    middle = flat_tokens + branch
    normed_mlp = lower_half(rms_norm(middle, gain_mlp_f))
    gate_up = low_back(jnp.dot(normed_mlp, w_gate_up_f, precision=highest))
    hidden = lower_half(jax.nn.silu(gate_up[:, :FF]) * gate_up[:, FF:])
    mlp_out = low_back(jnp.dot(hidden, w_down_f.T, precision=highest))
    return (middle + mlp_out).reshape(tokens_f.shape)

def reference(tokens, positions, block_order, w_qkv, qkv_bias, w_out, w_gate_up, w_down, gain_attn, gain_mlp, cotangent):
    cosine_table, sine_values = rope_tables(positions.reshape(-1))
    inverse_order = jnp.argsort(block_order).astype(jnp.int32)

    def forward(tokens_f, w_qkv_f, bias_f, w_out_f, w_gate_up_f, w_down_f, gain_attn_f, gain_mlp_f):
        return decoder_layer(tokens_f, w_qkv_f, bias_f, w_out_f, w_gate_up_f, w_down_f, gain_attn_f, gain_mlp_f, cosine_table, sine_values, block_order, inverse_order)
    output, pullback = jax.vjp(forward, tokens.astype(jnp.float32), w_qkv.astype(jnp.float32), qkv_bias.astype(jnp.float32), w_out.astype(jnp.float32), w_gate_up.astype(jnp.float32), w_down.astype(jnp.float32), gain_attn.astype(jnp.float32), gain_mlp.astype(jnp.float32))
    gradients = pullback(cotangent.astype(jnp.float32))
    return (output.astype(jnp.bfloat16), gradients[0].astype(jnp.bfloat16), gradients[1], gradients[2], gradients[3], gradients[4], gradients[5], gradients[6], gradients[7])
```

```python
import jax
import jax.numpy as jnp
from jax import lax
from jax.sharding import Mesh, PartitionSpec as P

QUERY_HEADS = 12
KEY_VALUE_HEADS = 2
HEAD_SIZE = 128
LANES = 128

norm_eps = 1e-06
rope_theta = 1000000.0
masked_score = -1e30

WIDE = ("wh", "wl")
GROUP = ("wl", "blk", "core")
PLANE = ("blk", "hx", "core")
f32, bf16 = jnp.float32, jnp.bfloat16


def rms_parts(values, gain_row):
    inverse = lax.rsqrt(jnp.mean(values * values, axis=-1, keepdims=True) + norm_eps)
    scaled = values * inverse
    return (scaled * gain_row, scaled, inverse)


def rms_back(grad_normed, scaled, inverse, gain_row):
    grad_scaled = grad_normed * gain_row
    mean_term = jnp.mean(grad_scaled * scaled, axis=-1, keepdims=True)
    return (inverse * (grad_scaled - scaled * mean_term), jnp.sum(grad_normed * scaled, axis=0))


def half_turn(values):
    half_size = values.shape[-1] // 2
    return jnp.concatenate([-values[..., half_size:], values[..., :half_size]], axis=-1)


def rotate_pairs(values, cosine_table, sine_values):
    return values * cosine_table + half_turn(values) * sine_values


def turn_back(values, cosine_table, sine_values):
    return values * cosine_table - half_turn(values * sine_values)


def rope_tables(positions):
    frequency = rope_theta ** (-jnp.arange(0, HEAD_SIZE, 2).astype(f32) / HEAD_SIZE)
    angles = positions.astype(f32)[:, None] * frequency[None, :]
    angles = jnp.concatenate([angles, angles], axis=-1)
    return (jnp.cos(angles), jnp.sin(angles))


def dot(a, b):
    return jnp.dot(a, b, preferred_element_type=f32)


def dot_rows(a, b):
    return lax.dot_general(a, b, (((0,), (0,)), ((), ())), preferred_element_type=f32)


def dot_cols(a, b):
    return lax.dot_general(a, b, (((1,), (1,)), ((), ())), preferred_element_type=f32)


def partner(values, axis, distance=1):
    count = lax.axis_size(axis)
    return lax.ppermute(values, axis, [(i, i ^ distance) for i in range(count)])


def shifted(values, axis, distance):
    count = lax.axis_size(axis)
    return lax.ppermute(values, axis, [((i + distance) % count, i) for i in range(count)])


def in_order(pieces, index):
    bit = 1
    while bit < len(pieces):
        odd = (index & bit) != 0
        pieces = [jnp.where(odd, pieces[k ^ bit], pieces[k]) for k in range(len(pieces))]
        bit *= 2
    return pieces


def gather_wide(own_by_parity, wide_index):
    count = lax.axis_size(WIDE)
    pieces = [own_by_parity[0]]
    for distance in range(1, count):
        pieces.append(partner(own_by_parity[(distance & 1) % len(own_by_parity)], WIDE, distance))
    return jnp.concatenate(in_order(pieces, wide_index), axis=0)


def on_device(
    tokens,
    positions,
    block_order,
    w_qkv,
    qkv_bias,
    w_out,
    w_gate_up,
    w_down,
    gain_attn,
    gain_mlp,
    cotangent,
):
    slot_count, seq_count, rows_dev, width = tokens.shape
    blk_count, x_count, core_count = (lax.axis_size(a) for a in ("blk", "hx", "core"))
    wide_count = lax.axis_size(WIDE)
    wide_at, wl_at, blk_at, x_at, core_at = (
        lax.axis_index(a) for a in (WIDE, "wl", "blk", "hx", "core")
    )
    head_at = x_at * core_count + core_at
    head_shards = x_count * core_count
    q_here = QUERY_HEADS // head_shards * HEAD_SIZE
    heads_here = QUERY_HEADS // head_shards
    q_total = QUERY_HEADS * HEAD_SIZE
    kv_total = KEY_VALUE_HEADS * HEAD_SIZE
    kv_at = head_at * KEY_VALUE_HEADS // head_shards
    rows_wide = w_qkv.shape[0]
    block_rows = rows_dev * head_shards
    dev_rows = slot_count * seq_count * rows_dev
    blk_rows = dev_rows * head_shards
    ff = w_down.shape[1]
    score_scale = HEAD_SIZE ** (-0.5)

    def gather_head(values):
        pair = jnp.stack([values, partner(values, "hx")])
        other = partner(pair, "core")
        return jnp.stack(in_order([pair, other], core_at))

    def block_major(values):
        return jnp.moveaxis(values, (0, 1), (2, 3))

    small = jnp.concatenate([qkv_bias, gain_attn, gain_mlp])[None]
    small = gather_wide([small], wide_at)
    bias_len = qkv_bias.shape[0]
    bias_row = small[:, :bias_len].reshape(1, -1).astype(f32)
    gain_attn_row = small[:, bias_len : bias_len + rows_wide].reshape(1, -1).astype(f32)
    gain_mlp_row = small[:, bias_len + rows_wide :].reshape(1, -1).astype(f32)

    def head_columns(array):
        return jnp.concatenate(
            [
                lax.dynamic_slice_in_dim(array, head_at * q_here, q_here, 1),
                lax.dynamic_slice_in_dim(array, q_total + kv_at * HEAD_SIZE, HEAD_SIZE, 1),
                lax.dynamic_slice_in_dim(
                    array, q_total + kv_total + kv_at * HEAD_SIZE, HEAD_SIZE, 1
                ),
            ],
            axis=1,
        )

    w_head = gather_wide([head_columns(w_qkv)], wide_at)
    bias_head = head_columns(bias_row)

    share = 2 * blk_count * core_count
    main = ff // (LANES * share) * LANES
    rest = ff // share - main

    def ff_columns(parity):
        at = ((wl_at ^ parity) * blk_count + blk_at) * core_count + core_at
        gate_main, rest_main = at * main, share * main + at * rest
        down = [
            lax.dynamic_slice_in_dim(w_down, gate_main, main, 1),
            lax.dynamic_slice_in_dim(w_down, rest_main, rest, 1),
        ]
        gate_up = [
            lax.dynamic_slice_in_dim(w_gate_up, gate_main, main, 1),
            lax.dynamic_slice_in_dim(w_gate_up, ff + gate_main, main, 1),
            lax.dynamic_slice_in_dim(w_gate_up, rest_main, rest, 1),
            lax.dynamic_slice_in_dim(w_gate_up, ff + rest_main, rest, 1),
        ]
        return jnp.concatenate(down + gate_up, axis=1)

    flat_tokens = tokens.reshape(-1, width)
    blk_tokens = block_major(gather_head(tokens)).reshape(-1, width)
    blk_positions = block_major(gather_head(positions)).reshape(-1)
    w_out_half = lax.dynamic_slice_in_dim(
        w_out, core_at * (rows_wide // 2), rows_wide // 2, 0
    )
    out_pieces = [w_out]
    for distance in range(1, wide_count):
        mine = partner(w_out_half, WIDE, distance)
        out_pieces.append(
            jnp.concatenate(in_order([mine, partner(mine, "core")], core_at), axis=0)
        )
    full_out = jnp.concatenate(in_order(out_pieces, wide_at), axis=0)
    w_out_head = lax.dynamic_slice_in_dim(full_out, head_at * q_here, q_here, 1)

    w_ff = gather_wide([ff_columns(0), ff_columns(1)], wide_at)
    w_down_here = w_ff[:, : main + rest]
    w_gate_up_here = w_ff[:, main + rest :]

    group_cotangent = lax.all_gather(
        cotangent.reshape(-1, width), GROUP, axis=0, tiled=True
    )

    normed_attn = rms_parts(blk_tokens.astype(f32), gain_attn_row)[0].astype(bf16)
    projected = dot(normed_attn, w_head) + bias_head
    cosine_table, sine_values = rope_tables(blk_positions)
    queries = (
        rotate_pairs(
            projected[:, :q_here].reshape(-1, heads_here, HEAD_SIZE),
            cosine_table[:, None, :],
            sine_values[:, None, :],
        )
        .astype(bf16)
        .reshape(slot_count, seq_count, block_rows, heads_here, HEAD_SIZE)
    )
    keys = rotate_pairs(projected[:, q_here : q_here + HEAD_SIZE], cosine_table, sine_values)
    pair = [keys.astype(bf16), projected[:, q_here + HEAD_SIZE :].astype(bf16)]
    sent = jnp.where(core_at == 0, pair[0], pair[1])
    arrived = jnp.stack([shifted(sent, "blk", d) for d in range(1, blk_count)])
    other = partner(arrived, "core")
    kv_shape = (blk_count * slot_count, seq_count, block_rows, HEAD_SIZE)
    all_keys, all_values = (
        jnp.concatenate([own[None], far]).reshape(kv_shape)
        for own, far in zip(pair, in_order([arrived, other], core_at))
    )
    key_slots = (
        (blk_at + jnp.arange(blk_count, dtype=jnp.int32)) % blk_count * slot_count
    )[:, None] + jnp.arange(slot_count, dtype=jnp.int32)[None]
    key_order = jnp.take(block_order, key_slots.reshape(-1))
    query_order = key_order[:slot_count]
    row_ids = (
        (2 * (jnp.arange(2, dtype=jnp.int32) ^ x_at))[None, :, None]
        + jnp.arange(2, dtype=jnp.int32)[:, None, None]
    ) * rows_dev + jnp.arange(rows_dev, dtype=jnp.int32)[None, None]
    row_ids = row_ids.reshape(-1)
    allowed = (key_order[None, :] < query_order[:, None])[:, None, None, :, None] | (
        (key_order[None, :] == query_order[:, None])[:, None, None, :, None]
        & (row_ids[None, :] <= row_ids[:, None])[None, :, None, None, :]
    )
    allowed = allowed[:, None]
    scores = (
        jnp.einsum("asrhd,kscd->asrhkc", queries, all_keys, preferred_element_type=f32)
        * score_scale
    )
    masked = jnp.where(allowed, scores, masked_score)
    peak = jnp.max(masked, axis=(-2, -1), keepdims=True)
    weights = jnp.exp(masked - peak)
    total = jnp.sum(weights, axis=(-2, -1), keepdims=True)
    log_total = peak + jnp.log(total)
    attention = jnp.einsum(
        "asrhkc,kscd->asrhd",
        (weights / total).astype(bf16),
        all_values,
        preferred_element_type=f32,
    )
    attended_head = attention.astype(bf16).reshape(blk_rows, q_here)

    back = attended_head.reshape(slot_count, seq_count, 2, 2, rows_dev, q_here)
    from_x = partner(back[:, :, :, 1], "hx")
    by_x = jnp.stack([back[:, :, :, 0], from_x])
    own_c, other_c = in_order([by_x[:, :, :, 0], by_x[:, :, :, 1]], core_at)
    by_core = in_order([own_c, partner(other_c, "core")], core_at)
    by_head = [
        piece for x_piece in zip(*(in_order(list(p), x_at) for p in by_core)) for piece in x_piece
    ]
    attended = jnp.concatenate(by_head, axis=-1).reshape(dev_rows, q_total)
    middle = flat_tokens.astype(f32) + dot_cols(attended, full_out)
    normed_mlp, scaled_mlp, inverse_mlp = rms_parts(middle, gain_mlp_row)
    normed_mlp = normed_mlp.astype(bf16)

    group_normed = lax.all_gather(normed_mlp, GROUP, axis=0, tiled=True)
    grad_hidden = dot(group_cotangent, w_down_here)
    gate_up = dot(group_normed, w_gate_up_here)

    def parts(values):
        return (
            (values[:, :main], values[:, main : 2 * main]),
            (values[:, 2 * main : 2 * main + rest], values[:, 2 * main + rest :]),
        )

    def gated(gate, up, grad):
        sigmoid = jax.nn.sigmoid(gate)
        silu = gate * sigmoid
        return (
            (silu * up).astype(bf16),
            (grad * up * sigmoid * (1.0 + gate * (1.0 - sigmoid))).astype(bf16),
            (grad * silu).astype(bf16),
        )

    (gate_m, up_m), (gate_r, up_r) = parts(gate_up)
    hidden_m, gg_m, gu_m = gated(gate_m, up_m, grad_hidden[:, :main])
    hidden_r, gg_r, gu_r = gated(gate_r, up_r, grad_hidden[:, main:])
    hidden = jnp.concatenate([hidden_m, hidden_r], axis=1)
    grad_gate_up = jnp.concatenate([gg_m, gu_m, gg_r, gu_r], axis=1)
    grad_normed_part = dot_cols(grad_gate_up, w_gate_up_here).astype(bf16)
    mlp_part = dot_cols(hidden, w_down_here).astype(bf16)
    grad_normed_mlp = lax.psum_scatter(
        grad_normed_part, GROUP, scatter_dimension=0, tiled=True
    ).astype(f32)

    ff_grad = jnp.concatenate(
        [dot_rows(group_cotangent, hidden), dot_rows(group_normed, grad_gate_up)], axis=1
    ).astype(bf16)
    half = rows_wide // 2
    halves = ff_grad.reshape(wide_count, 2, half, -1)
    mine, theirs = in_order([halves[:, 0], halves[:, 1]], x_at)
    ff_sum = mine.astype(f32) + partner(theirs, "hx").astype(f32)
    ff_send = ff_sum.astype(bf16)
    by_parity = [None, None]
    for distance in range(wide_count):
        rows_of = lax.dynamic_index_in_dim(ff_send, wide_at ^ distance, 0, keepdims=False)
        term = rows_of if distance == 0 else partner(rows_of, WIDE, distance)
        term = term.astype(f32)
        kept = by_parity[distance & 1]
        by_parity[distance & 1] = term if kept is None else kept + term
    ff_done = jnp.stack(in_order(by_parity, wl_at)).astype(bf16)
    ff_all = lax.all_gather(ff_done, PLANE, axis=0)
    ff_all = ff_all.reshape(blk_count, x_count, core_count, 2, half, -1)

    mlp_out = lax.psum_scatter(mlp_part, GROUP, scatter_dimension=0, tiled=True).astype(f32)
    output = (middle + mlp_out).astype(bf16).reshape(tokens.shape)

    grad_middle_part, grad_gain_mlp = rms_back(
        grad_normed_mlp, scaled_mlp, inverse_mlp, gain_mlp_row
    )
    grad_middle = cotangent.reshape(-1, width).astype(f32) + grad_middle_part
    grad_branch = grad_middle.astype(bf16)
    blk_branch = block_major(gather_head(grad_branch.reshape(tokens.shape))).reshape(-1, width)
    out_grad_part = dot_rows(blk_branch, attended_head)
    grad_heads = (
        dot(blk_branch, w_out_head)
        .astype(bf16)
        .reshape(slot_count, seq_count, block_rows, heads_here, HEAD_SIZE)
    )
    row_inner = jnp.sum(grad_heads.astype(f32) * attention, axis=-1)
    probs = jnp.exp(masked - log_total)
    grad_probs = jnp.einsum(
        "asrhd,kscd->asrhkc", grad_heads, all_values, preferred_element_type=f32
    )
    grad_scores = (probs * (grad_probs - row_inner[..., None, None])).astype(bf16)
    grad_queries = (
        jnp.einsum("asrhkc,kscd->asrhd", grad_scores, all_keys, preferred_element_type=f32)
        * score_scale
    )
    grad_keys = (
        jnp.einsum("asrhkc,asrhd->kscd", grad_scores, queries, preferred_element_type=f32)
        * score_scale
    )
    grad_values = jnp.einsum(
        "asrhkc,asrhd->kscd", probs.astype(bf16), grad_heads, preferred_element_type=f32
    )
    kept, given = in_order([grad_keys, grad_values], core_at)
    kept = kept + partner(given.astype(bf16), "core").astype(f32)
    kept = kept.reshape(blk_count, blk_rows, HEAD_SIZE)
    grad_pair = kept[0]
    for distance in range(1, blk_count):
        grad_pair = grad_pair + shifted(
            kept[blk_count - distance].astype(bf16), "blk", distance
        ).astype(f32)
    grad_pair = jnp.where(
        core_at == 0, turn_back(grad_pair, cosine_table, sine_values), grad_pair
    )
    grad_projected = jnp.concatenate(
        [
            turn_back(
                grad_queries.reshape(-1, heads_here, HEAD_SIZE),
                cosine_table[:, None, :],
                sine_values[:, None, :],
            ).reshape(-1, q_here),
            grad_pair,
        ],
        axis=1,
    ).astype(bf16)
    w_back = jnp.concatenate(
        [
            w_head[:, :q_here],
            jnp.where(
                core_at == 0,
                w_head[:, q_here : q_here + HEAD_SIZE],
                w_head[:, q_here + HEAD_SIZE :],
            ),
        ],
        axis=1,
    )
    back_part = dot_cols(grad_projected, w_back).astype(bf16)
    back_part = back_part.reshape(slot_count, seq_count, 2, 2, rows_dev, width)
    own_c, other_c = in_order([back_part[:, :, 0], back_part[:, :, 1]], core_at)
    own_c = own_c.astype(f32) + partner(other_c, "core").astype(f32)
    grad_normed_attn = own_c[:, :, 0] + partner(own_c[:, :, 1].astype(bf16), "hx").astype(f32)
    grad_normed_attn = grad_normed_attn.reshape(-1, width)
    scaled_attn, inverse_attn = rms_parts(flat_tokens.astype(f32), gain_attn_row)[1:]
    grad_flat, grad_gain_attn = rms_back(
        grad_normed_attn, scaled_attn, inverse_attn, gain_attn_row
    )
    input_grad = (grad_middle + grad_flat).astype(bf16).reshape(tokens.shape)

    column_sums = jnp.sum(grad_projected.astype(f32), axis=0)
    bias_sum = jnp.zeros((q_total + 2 * kv_total,), f32)
    bias_sum = lax.dynamic_update_slice(bias_sum, column_sums[:q_here], (head_at * q_here,))
    bias_sum = lax.dynamic_update_slice(
        bias_sum,
        column_sums[q_here:],
        (q_total + core_at * kv_total + kv_at * HEAD_SIZE,),
    )
    sums = jnp.concatenate([bias_sum, grad_gain_attn, grad_gain_mlp]).reshape(-1, LANES)
    for axis in ("core", "hx", "blk", "wl", "wh"):
        step = 1
        while step < lax.axis_size(axis):
            sums = sums + partner(sums, axis, step)
            step *= 2
    sums = sums.reshape(-1)
    bias_at = q_total + 2 * kv_total
    bias_grad = lax.dynamic_slice_in_dim(sums, wide_at * bias_len, bias_len)
    gain_attn_grad = lax.dynamic_slice_in_dim(sums, bias_at + wide_at * rows_wide, rows_wide)
    gain_mlp_grad = lax.dynamic_slice_in_dim(
        sums, bias_at + width + wide_at * rows_wide, rows_wide
    )

    proj_part = jnp.concatenate(
        [dot_rows(normed_attn, grad_projected), out_grad_part], axis=1
    ).astype(bf16)
    proj_done = lax.psum_scatter(
        proj_part, WIDE + ("blk",), scatter_dimension=0, tiled=True
    )
    proj_all = lax.all_gather(proj_done, PLANE, axis=0)
    proj_all = proj_all.reshape(blk_count, x_count, core_count, rows_wide // blk_count, -1)
    proj_q = proj_all[..., :q_here].transpose(0, 3, 1, 2, 4).reshape(rows_wide, q_total)
    proj_kv = proj_all[..., q_here : q_here + HEAD_SIZE]
    proj_kv = proj_kv.transpose(0, 3, 2, 1, 4).reshape(rows_wide, 2 * kv_total)
    proj_o = proj_all[..., q_here + HEAD_SIZE :].transpose(0, 3, 1, 2, 4)
    qkv_grad = jnp.concatenate([proj_q, proj_kv], axis=1).astype(f32)
    out_grad = proj_o.reshape(rows_wide, q_total).astype(f32)

    def columns(first, size):
        piece = ff_all[..., first : first + size]
        return piece.transpose(1, 4, 3, 0, 2, 5).reshape(rows_wide, share * size)

    at = main + rest
    down_grad = jnp.concatenate([columns(0, main), columns(main, rest)], axis=1).astype(f32)
    gate_up_grad = jnp.concatenate(
        [
            columns(at, main),
            columns(at + 2 * main, rest),
            columns(at + main, main),
            columns(at + 2 * main + rest, rest),
        ],
        axis=1,
    ).astype(f32)
    return (
        output,
        input_grad,
        qkv_grad,
        bias_grad,
        out_grad,
        gate_up_grad,
        down_grad,
        gain_attn_grad,
        gain_mlp_grad,
    )


def solution(mesh):
    wide, blk, head = mesh.devices.shape
    cores = 2
    fine = Mesh(
        mesh.devices.reshape(wide // 2, 2, blk, head // cores, cores),
        ("wh", "wl", "blk", "hx", "core"),
    )
    rows = P("blk", WIDE, ("hx", "core"), None)
    matrix, vector = P(WIDE, None), P(WIDE)
    in_specs = (
        rows,
        P("blk", WIDE, ("hx", "core")),
        P(),
        matrix,
        vector,
        matrix,
        matrix,
        matrix,
        vector,
        vector,
        rows,
    )
    out_specs = (rows, rows, matrix, vector, matrix, matrix, matrix, vector, vector)
    return jax.shard_map(
        on_device, mesh=fine, in_specs=in_specs, out_specs=out_specs, check_vma=False
    )
```

```python
import jax
import jax.numpy as jnp
from jax import lax
from jax.sharding import Mesh, PartitionSpec as P

QUERY_HEADS = 12
KEY_VALUE_HEADS = 2
HEAD_SIZE = 128
LANES = 128

norm_eps = 1e-06
rope_theta = 1000000.0
masked_score = -1e30

WIDE = "wide"
PLANE = ("blk", "hx", "core")
f32, bf16 = jnp.float32, jnp.bfloat16


def rms_parts(values, gain_row):
    inverse = lax.rsqrt(jnp.mean(values * values, axis=-1, keepdims=True) + norm_eps)
    scaled = values * inverse
    return (scaled * gain_row, scaled, inverse)


def rms_back(grad_normed, scaled, inverse, gain_row):
    grad_scaled = grad_normed * gain_row
    mean_term = jnp.mean(grad_scaled * scaled, axis=-1, keepdims=True)
    return (inverse * (grad_scaled - scaled * mean_term), jnp.sum(grad_normed * scaled, axis=0))


def turn_back(values, cosine_table, sine_values):
    half_size = values.shape[-1] // 2
    turned = values * sine_values
    turned = jnp.concatenate([turned[..., half_size:], turned[..., :half_size]], axis=-1)
    return values * cosine_table + turned


def rope_tables(positions):
    frequency = rope_theta ** (-jnp.arange(0, HEAD_SIZE, 2).astype(f32) / HEAD_SIZE)
    angles = positions.astype(f32)[:, None] * frequency[None, :]
    cosine, sine = jnp.cos(angles), jnp.sin(angles)
    return (
        jnp.concatenate([cosine, cosine], axis=-1),
        jnp.concatenate([-sine, sine], axis=-1),
    )


def dot(a, b):
    return jnp.dot(a, b, preferred_element_type=f32)


def dot_rows(a, b):
    return lax.dot_general(a, b, (((0,), (0,)), ((), ())), preferred_element_type=f32)


def dot_cols(a, b):
    return lax.dot_general(a, b, (((1,), (1,)), ((), ())), preferred_element_type=f32)


def partner(values, axis, distance=1):
    count = lax.axis_size(axis)
    return lax.ppermute(values, axis, [(i, i ^ distance) for i in range(count)])


def shifted(values, axis, distance):
    count = lax.axis_size(axis)
    return lax.ppermute(values, axis, [((i + distance) % count, i) for i in range(count)])


def in_order(pieces, index):
    bit = 1
    while bit < len(pieces):
        odd = (index & bit) != 0
        pieces = [jnp.where(odd, pieces[k ^ bit], pieces[k]) for k in range(len(pieces))]
        bit *= 2
    return pieces


def row_places(index, x_at, rows_dev):
    x_rel = (index // rows_dev) % 2
    core = index // (2 * rows_dev)
    x_abs = jnp.where(x_at == 0, x_rel, 1 - x_rel)
    return (2 * x_abs + core) * rows_dev + index % rows_dev


def on_device(
    tokens,
    positions,
    block_order,
    w_qkv,
    qkv_bias,
    w_out,
    w_gate_up,
    w_down,
    gain_attn,
    gain_mlp,
    cotangent,
):
    slot_count, seq_count, rows_dev, width = tokens.shape
    blk_count, x_count, core_count = (lax.axis_size(a) for a in ("blk", "hx", "core"))
    wide_count = lax.axis_size(WIDE)
    wide_at, blk_at, x_at, core_at = (lax.axis_index(a) for a in (WIDE, "blk", "hx", "core"))
    head_at = x_at * core_count + core_at
    head_shards = x_count * core_count
    heads_here = QUERY_HEADS // head_shards
    q_here = heads_here * HEAD_SIZE
    q_total = QUERY_HEADS * HEAD_SIZE
    kv_total = KEY_VALUE_HEADS * HEAD_SIZE
    kv_at = head_at * KEY_VALUE_HEADS // head_shards
    rows_wide = w_qkv.shape[0]
    half = rows_wide // 2
    block_rows = rows_dev * head_shards
    dev_rows = slot_count * seq_count * rows_dev
    blk_rows = dev_rows * head_shards
    ff = w_down.shape[1]
    others = range(1, wide_count)

    def by_wide(own, pieces):
        return jnp.concatenate(in_order([own] + pieces, wide_at), axis=0)

    def block_major(near, far):
        return jnp.moveaxis(jnp.stack(in_order([near, far], core_at)), (0, 1), (2, 3))

    def head_columns(array):
        return jnp.concatenate(
            [
                lax.dynamic_slice_in_dim(array, head_at * q_here, q_here, 1),
                lax.dynamic_slice_in_dim(array, q_total + kv_at * HEAD_SIZE, HEAD_SIZE, 1),
                lax.dynamic_slice_in_dim(
                    array, q_total + kv_total + kv_at * HEAD_SIZE, HEAD_SIZE, 1
                ),
            ],
            axis=1,
        )

    share = blk_count * x_count * core_count
    main = ff // (LANES * share) * LANES
    extra = (ff - share * main) // LANES
    ff_here = main + LANES

    def ff_columns():
        at = blk_at * x_count + x_at
        has = (core_at == 0) & (at < extra)
        columns = []
        for array, first in ((w_down, 0), (w_gate_up, 0), (w_gate_up, ff)):
            more = lax.dynamic_slice_in_dim(array, first + share * main + at * LANES, LANES, 1)
            columns += [
                lax.dynamic_slice_in_dim(
                    array, first + (at * core_count + core_at) * main, main, 1
                ),
                jnp.where(has, more, jnp.zeros_like(more)),
            ]
        return jnp.concatenate(columns, axis=1)

    tokens_x = partner(tokens, "hx")
    positions_x = partner(positions, "hx")
    small = jnp.concatenate([qkv_bias, gain_attn, gain_mlp])[None]
    small = by_wide(small, [partner(small, WIDE, d) for d in others])
    w_head_own = head_columns(w_qkv)
    w_head_far = [partner(w_head_own, WIDE, d) for d in others]
    cot_rows = cotangent.reshape(-1, width)
    group_cotangent = lax.all_gather(cot_rows, PLANE, axis=0, tiled=True)
    w_out_half = lax.dynamic_slice_in_dim(w_out, core_at * half, half, 0)
    w_out_far = [partner(w_out_half, WIDE, d) for d in others]
    bias_len = qkv_bias.shape[0]
    bias_row = small[:, :bias_len].reshape(1, -1).astype(f32)
    gain_attn_row = small[:, bias_len : bias_len + rows_wide].reshape(1, -1).astype(f32)
    gain_mlp_row = small[:, bias_len + rows_wide :].reshape(1, -1).astype(f32)

    tokens_pair = jnp.stack([tokens, tokens_x])
    positions_pair = jnp.stack([positions, positions_x])
    blk_tokens = block_major(tokens_pair, partner(tokens_pair, "core")).reshape(-1, width)
    blk_positions = block_major(positions_pair, partner(positions_pair, "core")).reshape(-1)
    cosine_table, sine_values = rope_tables(blk_positions)
    w_head = by_wide(w_head_own, w_head_far)
    normed_attn = rms_parts(blk_tokens.astype(f32), gain_attn_row)[0].astype(bf16)
    projected = dot(normed_attn, w_head) + head_columns(bias_row)

    def turned(values):
        moved = jnp.concatenate(
            [values[..., HEAD_SIZE // 2 :], values[..., : HEAD_SIZE // 2]], axis=-1
        )
        return (values * cosine_table[:, None] + moved * sine_values[:, None]).astype(bf16)

    queries = turned(projected[:, :q_here].reshape(-1, heads_here, HEAD_SIZE)).reshape(-1, q_here)
    own_keys = turned(projected[:, None, q_here : q_here + HEAD_SIZE])[:, 0]
    own_values = projected[:, q_here + HEAD_SIZE :].astype(bf16)
    pair = [own_keys, own_values]
    sent = jnp.where(core_at == 0, pair[0], pair[1])
    ff_own = ff_columns()
    ff_far = [partner(ff_own, WIDE, d) for d in others]
    arrived = [shifted(sent, "blk", d) for d in range(1, blk_count)]
    arrived = jnp.stack(arrived)
    other = partner(arrived, "core")
    kv_shape = (blk_count * slot_count, seq_count, block_rows, HEAD_SIZE)
    all_keys, all_values = (
        jnp.concatenate([own[None], far]).reshape(kv_shape)
        for own, far in zip(pair, in_order([arrived, other], core_at))
    )
    key_slots = (
        (blk_at + jnp.arange(blk_count, dtype=jnp.int32)) % blk_count * slot_count
    )[:, None] + jnp.arange(slot_count, dtype=jnp.int32)[None]
    key_order = jnp.take(block_order, key_slots.reshape(-1))

    query_order = key_order[:slot_count]
    places = row_places(jnp.arange(block_rows, dtype=jnp.int32), x_at, rows_dev)
    queries = queries.reshape(slot_count, seq_count, block_rows, heads_here, HEAD_SIZE)
    scale = HEAD_SIZE**-0.5
    allowed = (
        places[None, None, None, None, None, :]
        <= places[None, None, :, None, None, None]
        + (query_order[:, None] - key_order[None, :])[:, None, None, None, :, None] * block_rows
    )
    scores = jnp.einsum("asrhd,kscd->asrhkc", queries, all_keys, preferred_element_type=f32)
    masked = jnp.where(allowed, scores * scale, masked_score)
    peak = jnp.max(masked, axis=(-2, -1), keepdims=True)
    weights = jnp.exp(masked - peak)
    total = jnp.sum(weights, axis=(-2, -1), keepdims=True)
    log_total = peak + jnp.log(total)
    attention = jnp.einsum(
        "asrhkc,kscd->asrhd", (weights / total).astype(bf16), all_values, preferred_element_type=f32
    )
    attended_head = attention.astype(bf16).reshape(blk_rows, q_here)
    back = attended_head.reshape(slot_count, seq_count, 2, 2, rows_dev, q_here)
    back_x = back[:, :, :, 1]
    from_x = partner(back_x, "hx")

    out_far = [
        jnp.concatenate(in_order([far, partner(far, "core")], core_at), axis=0)
        for far in w_out_far
    ]
    full_out = by_wide(w_out, out_far)
    w_out_head = lax.dynamic_slice_in_dim(full_out, head_at * q_here, q_here, 1)
    w_ff = by_wide(ff_own, ff_far)

    by_x = jnp.stack([back[:, :, :, 0], from_x])
    own_c, other_c = in_order([by_x[:, :, :, 0], by_x[:, :, :, 1]], core_at)
    by_core = in_order([own_c, partner(other_c, "core")], core_at)
    by_head = [
        piece for x_piece in zip(*(in_order(list(p), x_at) for p in by_core)) for piece in x_piece
    ]
    attended = jnp.concatenate(by_head, axis=-1).reshape(dev_rows, q_total)
    flat_tokens = tokens.reshape(-1, width).astype(f32)
    middle = flat_tokens + dot_cols(attended, full_out)
    normed_mlp = rms_parts(middle, gain_mlp_row)[0].astype(bf16)

    normed_mlp, group_cotangent = lax.optimization_barrier((normed_mlp, group_cotangent))
    group_normed = lax.all_gather(normed_mlp, PLANE, axis=0, tiled=True)
    w_down_here, w_gate_up_here = w_ff[:, :ff_here], w_ff[:, ff_here:]
    grad_hidden = dot(group_cotangent, w_down_here)
    gate_up = dot(group_normed, w_gate_up_here)
    gate, up = gate_up[:, :ff_here], gate_up[:, ff_here:]
    sigmoid = jax.nn.sigmoid(gate)
    silu = gate * sigmoid
    hidden = (silu * up).astype(bf16)
    grad_gate = (grad_hidden * up * (sigmoid + silu * (1.0 - sigmoid))).astype(bf16)
    grad_up = (grad_hidden * silu).astype(bf16)
    grad_gate_up = jnp.concatenate([grad_gate, grad_up], axis=1)
    grad_part = dot_cols(grad_gate_up, w_gate_up_here).astype(bf16)
    grad_normed_mlp = lax.psum_scatter(grad_part, PLANE, scatter_dimension=0, tiled=True)
    down_part = dot_rows(group_cotangent, hidden).astype(bf16)
    gate_part = dot_rows(group_normed, grad_gate).astype(bf16)
    up_part = dot_rows(group_normed, grad_up).astype(bf16)

    def over_wide(part):
        parts = part.reshape(wide_count, rows_wide, -1)
        total = lax.dynamic_index_in_dim(parts, wide_at, 0, keepdims=False).astype(f32)
        for d in others:
            theirs = lax.dynamic_index_in_dim(parts, wide_at ^ d, 0, keepdims=False)
            total = total + partner(theirs, WIDE, d).astype(f32)
        return total.astype(bf16)

    sums_ff = [over_wide(part) for part in (down_part, gate_part, up_part)]
    grad_normed_mlp, *sums_ff = lax.optimization_barrier((grad_normed_mlp, *sums_ff))
    ff_all = lax.all_gather(
        jnp.concatenate(
            [total[:, :main] for total in sums_ff] + [total[:, main:] for total in sums_ff],
            axis=1,
        ),
        PLANE,
        axis=0,
    )

    _, scaled_mlp, inverse_mlp = rms_parts(middle, gain_mlp_row)
    grad_middle, grad_gain_mlp = rms_back(
        grad_normed_mlp.astype(f32), scaled_mlp, inverse_mlp, gain_mlp_row
    )
    grad_middle = cotangent.reshape(-1, width).astype(f32) + grad_middle
    grad_branch = grad_middle.astype(bf16).reshape(tokens.shape)
    branch_pair = jnp.stack([grad_branch, partner(grad_branch, "hx")])

    blk_branch = block_major(branch_pair, partner(branch_pair, "core")).reshape(-1, width)
    grad_heads = dot(blk_branch, w_out_head).astype(bf16)
    hidden, grad_heads = lax.optimization_barrier((hidden, grad_heads))
    out_part = dot_cols(hidden, w_down_here).astype(bf16)
    grad_heads = grad_heads.reshape(queries.shape)
    row_inner = jnp.sum(grad_heads.astype(f32) * attention, axis=-1)
    probs = jnp.exp(masked - log_total)
    grad_probs = jnp.einsum(
        "asrhd,kscd->asrhkc", grad_heads, all_values, preferred_element_type=f32
    )
    grad_scores = (probs * (grad_probs - row_inner[..., None, None])).astype(bf16)
    grad_queries = (
        jnp.einsum("asrhkc,kscd->asrhd", grad_scores, all_keys, preferred_element_type=f32) * scale
    )
    grad_queries = turn_back(
        grad_queries.reshape(-1, heads_here, HEAD_SIZE),
        cosine_table[:, None, :],
        sine_values[:, None, :],
    ).reshape(-1, q_here)
    grad_keys = (
        jnp.einsum("asrhkc,asrhd->kscd", grad_scores, queries, preferred_element_type=f32) * scale
    )
    grad_values = jnp.einsum(
        "asrhkc,asrhd->kscd", probs.astype(bf16), grad_heads, preferred_element_type=f32
    )
    kept, given = in_order([grad_keys, grad_values], core_at)
    kept = kept + partner(given.astype(bf16), "core").astype(f32)
    kept = kept.reshape(blk_count, blk_rows, HEAD_SIZE)
    sent_pair = [kept[blk_count - d].astype(bf16) for d in range(1, blk_count)]
    out_grad_part = dot_rows(blk_branch, attended_head)
    grad_pair = kept[0]
    for d in range(1, blk_count):
        grad_pair = grad_pair + shifted(sent_pair[d - 1], "blk", d).astype(f32)
    grad_pair = jnp.where(
        core_at == 0, turn_back(grad_pair, cosine_table, sine_values), grad_pair
    )
    grad_projected = jnp.concatenate([grad_queries, grad_pair], axis=1).astype(bf16)
    w_back = jnp.concatenate(
        [
            w_head[:, :q_here],
            jnp.where(
                core_at == 0,
                w_head[:, q_here : q_here + HEAD_SIZE],
                w_head[:, q_here + HEAD_SIZE :],
            ),
        ],
        axis=1,
    )
    back_part = dot_cols(grad_projected, w_back).astype(bf16)
    back_part = back_part.reshape(slot_count, seq_count, 2, 2, rows_dev, width)
    own_c, other_c = in_order([back_part[:, :, 0], back_part[:, :, 1]], core_at)

    qkv_part = dot_rows(normed_attn, grad_projected)
    proj_part = jnp.concatenate(
        [qkv_part[:, :q_here], out_grad_part, qkv_part[:, q_here:]], axis=1
    ).astype(bf16)
    proj_part = proj_part.reshape(wide_count, rows_wide, -1)
    proj_sum = lax.dynamic_index_in_dim(proj_part, wide_at, 0, keepdims=False).astype(f32)
    for d in others:
        theirs = lax.dynamic_index_in_dim(proj_part, wide_at ^ d, 0, keepdims=False)
        proj_sum = proj_sum + partner(theirs, WIDE, d).astype(f32)

    own_c = own_c.astype(f32) + partner(other_c, "core").astype(f32)
    given_x = own_c[:, :, 1].astype(bf16)
    grad_normed_attn = own_c[:, :, 0] + partner(given_x, "hx").astype(f32)
    proj_parts = proj_sum.reshape(blk_count, rows_wide // blk_count, -1)
    proj_done = lax.dynamic_index_in_dim(proj_parts, blk_at, 0, keepdims=False)
    for d in range(1, blk_count):
        theirs = lax.dynamic_index_in_dim(proj_parts, blk_at ^ d, 0, keepdims=False)
        proj_done = proj_done + partner(theirs.astype(bf16), "blk", d).astype(f32)
    grad_normed_attn = grad_normed_attn.reshape(-1, width)
    scaled_attn, inverse_attn = rms_parts(flat_tokens, gain_attn_row)[1:]
    grad_flat, grad_gain_attn = rms_back(
        grad_normed_attn, scaled_attn, inverse_attn, gain_attn_row
    )
    input_grad = (grad_middle + grad_flat).astype(bf16).reshape(tokens.shape)
    proj_done = proj_done.astype(bf16)
    proj_blk = [proj_done] + [partner(proj_done, "blk", d) for d in range(1, blk_count)]
    proj_rows = jnp.concatenate(in_order(proj_blk, blk_at))
    proj_rows, ff_all = lax.optimization_barrier((proj_rows, ff_all))
    proj_pair = jnp.stack(in_order([proj_rows, partner(proj_rows, "hx")], x_at))
    proj_all = in_order([proj_pair, partner(proj_pair, "core")], core_at)

    column_sums = jnp.sum(grad_projected.astype(f32), axis=0)
    bias_sum = jnp.zeros((q_total + 2 * kv_total,), f32)
    bias_sum = lax.dynamic_update_slice(bias_sum, column_sums[:q_here], (head_at * q_here,))
    bias_sum = lax.dynamic_update_slice(
        bias_sum,
        column_sums[q_here:],
        (q_total + core_at * kv_total + kv_at * HEAD_SIZE,),
    )
    sums = jnp.concatenate([bias_sum, grad_gain_attn, grad_gain_mlp.reshape(-1)]).reshape(-1, LANES)
    for axis in ("core", "hx", "blk", WIDE):
        step = 1
        while step < lax.axis_size(axis):
            sums = sums + partner(sums, axis, step)
            step *= 2
    sums = sums.reshape(-1)
    bias_at = q_total + 2 * kv_total
    bias_grad = lax.dynamic_slice_in_dim(sums, wide_at * bias_len, bias_len)
    gain_attn_grad = lax.dynamic_slice_in_dim(sums, bias_at + wide_at * rows_wide, rows_wide)
    gain_mlp_grad = lax.dynamic_slice_in_dim(
        sums, bias_at + width + wide_at * rows_wide, rows_wide
    )

    heads = [(x, c) for x in range(x_count) for c in range(core_count)]
    qkv_grad = jnp.concatenate(
        [proj_all[c][x, :, :q_here] for x, c in heads]
        + [proj_all[c][x, :, 2 * q_here :] for c in range(core_count) for x in range(x_count)],
        axis=1,
    ).astype(f32)
    out_grad = jnp.concatenate(
        [proj_all[c][x, :, q_here : 2 * q_here] for x, c in heads], axis=1
    ).astype(f32)

    def assembled(kinds):
        into = jnp.zeros((rows_wide, len(kinds) * ff), f32)
        at = 0
        for kind in kinds:
            pieces = [ff_all[p, :, kind * main : (kind + 1) * main] for p in range(share)]
            first = 3 * main + kind * LANES
            pieces += [ff_all[e * core_count, :, first : first + LANES] for e in range(extra)]
            for piece in pieces:
                into = lax.dynamic_update_slice(into, piece.astype(f32), (0, at))
                at += piece.shape[1]
        return into

    ff_all, out_part = lax.optimization_barrier((ff_all, out_part))
    down_grad, gate_up_grad = assembled([0]), assembled([1, 2])
    mlp_out = lax.psum_scatter(out_part, PLANE, scatter_dimension=0, tiled=True)
    output = (middle + mlp_out.astype(f32)).astype(bf16).reshape(tokens.shape)
    return (
        output,
        input_grad,
        qkv_grad,
        bias_grad,
        out_grad,
        gate_up_grad,
        down_grad,
        gain_attn_grad,
        gain_mlp_grad,
    )


def solution(mesh):
    wide, blk, head = mesh.devices.shape
    cores = 2
    fine = Mesh(
        mesh.devices.reshape(wide, blk, head // cores, cores), (WIDE, "blk", "hx", "core")
    )
    rows = P("blk", WIDE, ("hx", "core"), None)
    matrix, vector = P(WIDE, None), P(WIDE)
    in_specs = (
        rows,
        P("blk", WIDE, ("hx", "core")),
        P(),
        matrix,
        vector,
        matrix,
        matrix,
        matrix,
        vector,
        vector,
        rows,
    )
    out_specs = (rows, rows, matrix, vector, matrix, matrix, matrix, vector, vector)
    return jax.shard_map(
        on_device, mesh=fine, in_specs=in_specs, out_specs=out_specs, check_vma=False
    )
```

```python
import jax
import jax.numpy as jnp
from jax import lax
from jax.sharding import Mesh, PartitionSpec as P

QUERY_HEADS = 12
KEY_VALUE_HEADS = 2
HEAD_SIZE = 128
LANES = 128

norm_eps = 1e-06
rope_theta = 1000000.0
masked_score = -1e30

WIDE = "wide"
PLANE = ("blk", "hx", "core")
f32, bf16 = jnp.float32, jnp.bfloat16


def rms_parts(values, gain_row):
    inverse = lax.rsqrt(jnp.mean(values * values, axis=-1, keepdims=True) + norm_eps)
    scaled = values * inverse
    return (scaled * gain_row, scaled, inverse)


def rms_back(grad_normed, scaled, inverse, gain_row):
    grad_scaled = grad_normed * gain_row
    mean_term = jnp.mean(grad_scaled * scaled, axis=-1, keepdims=True)
    return (inverse * (grad_scaled - scaled * mean_term), jnp.sum(grad_normed * scaled, axis=0))


def turn_back(values, cosine_table, sine_values):
    half_size = values.shape[-1] // 2
    turned = values * sine_values
    turned = jnp.concatenate([turned[..., half_size:], turned[..., :half_size]], axis=-1)
    return values * cosine_table + turned


def rope_tables(positions):
    frequency = rope_theta ** (-jnp.arange(0, HEAD_SIZE, 2).astype(f32) / HEAD_SIZE)
    angles = positions.astype(f32)[:, None] * frequency[None, :]
    cosine, sine = jnp.cos(angles), jnp.sin(angles)
    return (
        jnp.concatenate([cosine, cosine], axis=-1),
        jnp.concatenate([-sine, sine], axis=-1),
    )


def dot(a, b):
    return jnp.dot(a, b, preferred_element_type=f32)


def dot_rows(a, b):
    return lax.dot_general(a, b, (((0,), (0,)), ((), ())), preferred_element_type=f32)


def dot_cols(a, b):
    return lax.dot_general(a, b, (((1,), (1,)), ((), ())), preferred_element_type=f32)


def partner(values, axis, distance=1):
    count = lax.axis_size(axis)
    return lax.ppermute(values, axis, [(i, i ^ distance) for i in range(count)])


def shifted(values, axis, distance):
    count = lax.axis_size(axis)
    return lax.ppermute(values, axis, [((i + distance) % count, i) for i in range(count)])


def in_order(pieces, index):
    bit = 1
    while bit < len(pieces):
        odd = (index & bit) != 0
        pieces = [jnp.where(odd, pieces[k ^ bit], pieces[k]) for k in range(len(pieces))]
        bit *= 2
    return pieces


def row_places(index, x_at, rows_dev):
    x_rel = (index // rows_dev) % 2
    core = index // (2 * rows_dev)
    x_abs = jnp.where(x_at == 0, x_rel, 1 - x_rel)
    return (2 * x_abs + core) * rows_dev + index % rows_dev


def on_device(
    tokens,
    positions,
    block_order,
    w_qkv,
    qkv_bias,
    w_out,
    w_gate_up,
    w_down,
    gain_attn,
    gain_mlp,
    cotangent,
):
    slot_count, seq_count, rows_dev, width = tokens.shape
    blk_count, x_count, core_count = (lax.axis_size(a) for a in ("blk", "hx", "core"))
    wide_count = lax.axis_size(WIDE)
    wide_at, blk_at, x_at, core_at = (lax.axis_index(a) for a in (WIDE, "blk", "hx", "core"))
    head_at = x_at * core_count + core_at
    head_shards = x_count * core_count
    heads_here = QUERY_HEADS // head_shards
    q_here = heads_here * HEAD_SIZE
    q_total = QUERY_HEADS * HEAD_SIZE
    kv_total = KEY_VALUE_HEADS * HEAD_SIZE
    kv_at = head_at * KEY_VALUE_HEADS // head_shards
    rows_wide = w_qkv.shape[0]
    half = rows_wide // 2
    block_rows = rows_dev * head_shards
    dev_rows = slot_count * seq_count * rows_dev
    blk_rows = dev_rows * head_shards
    ff = w_down.shape[1]
    others = range(1, wide_count)

    def by_wide(own, pieces):
        return jnp.concatenate(in_order([own] + pieces, wide_at), axis=0)

    def block_major(near, far):
        return jnp.moveaxis(jnp.stack(in_order([near, far], core_at)), (0, 1), (2, 3))

    def head_columns(array):
        return jnp.concatenate(
            [
                lax.dynamic_slice_in_dim(array, head_at * q_here, q_here, 1),
                lax.dynamic_slice_in_dim(array, q_total + kv_at * HEAD_SIZE, HEAD_SIZE, 1),
                lax.dynamic_slice_in_dim(
                    array, q_total + kv_total + kv_at * HEAD_SIZE, HEAD_SIZE, 1
                ),
            ],
            axis=1,
        )

    share = blk_count * x_count * core_count
    main = ff // (LANES * share) * LANES
    extra = (ff - share * main) // LANES
    ff_here = main + LANES

    def ff_columns():
        at = blk_at * x_count + x_at
        has = (core_at == 0) & (at < extra)
        columns = []
        for array, first in ((w_down, 0), (w_gate_up, 0), (w_gate_up, ff)):
            more = lax.dynamic_slice_in_dim(array, first + share * main + at * LANES, LANES, 1)
            columns += [
                lax.dynamic_slice_in_dim(
                    array, first + (at * core_count + core_at) * main, main, 1
                ),
                jnp.where(has, more, jnp.zeros_like(more)),
            ]
        return jnp.concatenate(columns, axis=1)

    tokens_x = partner(tokens, "hx")
    positions_x = partner(positions, "hx")
    small = jnp.concatenate([qkv_bias, gain_attn, gain_mlp])[None]
    small = by_wide(small, [partner(small, WIDE, d) for d in others])
    w_head_own = head_columns(w_qkv)
    w_head_far = [partner(w_head_own, WIDE, d) for d in others]
    cot_rows = cotangent.reshape(-1, width)
    group_cotangent = lax.all_gather(cot_rows, PLANE, axis=0, tiled=True)
    w_out_half = lax.dynamic_slice_in_dim(w_out, core_at * half, half, 0)
    w_out_far = [partner(w_out_half, WIDE, d) for d in others]
    bias_len = qkv_bias.shape[0]
    bias_row = small[:, :bias_len].reshape(1, -1).astype(f32)
    gain_attn_row = small[:, bias_len : bias_len + rows_wide].reshape(1, -1).astype(f32)
    gain_mlp_row = small[:, bias_len + rows_wide :].reshape(1, -1).astype(f32)

    tokens_pair = jnp.stack([tokens, tokens_x])
    positions_pair = jnp.stack([positions, positions_x])
    blk_tokens = block_major(tokens_pair, partner(tokens_pair, "core")).reshape(-1, width)
    blk_positions = block_major(positions_pair, partner(positions_pair, "core")).reshape(-1)
    cosine_table, sine_values = rope_tables(blk_positions)
    w_head = by_wide(w_head_own, w_head_far)
    normed_attn = rms_parts(blk_tokens.astype(f32), gain_attn_row)[0].astype(bf16)
    projected = dot(normed_attn, w_head) + head_columns(bias_row)

    def turned(values):
        moved = jnp.concatenate(
            [values[..., HEAD_SIZE // 2 :], values[..., : HEAD_SIZE // 2]], axis=-1
        )
        return (values * cosine_table[:, None] + moved * sine_values[:, None]).astype(bf16)

    queries = turned(projected[:, :q_here].reshape(-1, heads_here, HEAD_SIZE)).reshape(-1, q_here)
    own_keys = turned(projected[:, None, q_here : q_here + HEAD_SIZE])[:, 0]
    own_values = projected[:, q_here + HEAD_SIZE :].astype(bf16)
    pair = [own_keys, own_values]
    sent = jnp.where(core_at == 0, pair[0], pair[1])
    ff_own = ff_columns()
    ff_far = [partner(ff_own, WIDE, d) for d in others]
    arrived = [shifted(sent, "blk", d) for d in range(1, blk_count)]
    arrived = jnp.stack(arrived)
    other = partner(arrived, "core")
    kv_shape = (blk_count * slot_count, seq_count, block_rows, HEAD_SIZE)
    all_keys, all_values = (
        jnp.concatenate([own[None], far]).reshape(kv_shape)
        for own, far in zip(pair, in_order([arrived, other], core_at))
    )
    key_slots = (
        (blk_at + jnp.arange(blk_count, dtype=jnp.int32)) % blk_count * slot_count
    )[:, None] + jnp.arange(slot_count, dtype=jnp.int32)[None]
    key_order = jnp.take(block_order, key_slots.reshape(-1))

    query_order = key_order[:slot_count]
    places = row_places(jnp.arange(block_rows, dtype=jnp.int32), x_at, rows_dev)
    queries = queries.reshape(slot_count, seq_count, block_rows, heads_here, HEAD_SIZE)
    scale = HEAD_SIZE**-0.5
    allowed = (
        places[None, None, None, None, None, :]
        <= places[None, None, :, None, None, None]
        + (query_order[:, None] - key_order[None, :])[:, None, None, None, :, None] * block_rows
    )
    scores = jnp.einsum("asrhd,kscd->asrhkc", queries, all_keys, preferred_element_type=f32)
    masked = jnp.where(allowed, scores * scale, masked_score)
    peak = jnp.max(masked, axis=(-2, -1), keepdims=True)
    weights = jnp.exp(masked - peak)
    total = jnp.sum(weights, axis=(-2, -1), keepdims=True)
    log_total = peak + jnp.log(total)
    attention = jnp.einsum(
        "asrhkc,kscd->asrhd", (weights / total).astype(bf16), all_values, preferred_element_type=f32
    )
    attended_head = attention.astype(bf16).reshape(blk_rows, q_here)
    back = attended_head.reshape(slot_count, seq_count, 2, 2, rows_dev, q_here)
    back_x = back[:, :, :, 1]
    from_x = partner(back_x, "hx")

    out_far = [
        jnp.concatenate(in_order([far, partner(far, "core")], core_at), axis=0)
        for far in w_out_far
    ]
    full_out = by_wide(w_out, out_far)
    w_out_head = lax.dynamic_slice_in_dim(full_out, head_at * q_here, q_here, 1)
    w_ff = by_wide(ff_own, ff_far)

    by_x = jnp.stack([back[:, :, :, 0], from_x])
    own_c, other_c = in_order([by_x[:, :, :, 0], by_x[:, :, :, 1]], core_at)
    by_core = in_order([own_c, partner(other_c, "core")], core_at)
    by_head = [
        piece for x_piece in zip(*(in_order(list(p), x_at) for p in by_core)) for piece in x_piece
    ]
    attended = jnp.concatenate(by_head, axis=-1).reshape(dev_rows, q_total)
    flat_tokens = tokens.reshape(-1, width).astype(f32)
    middle = flat_tokens + dot_cols(attended, full_out)
    normed_mlp = rms_parts(middle, gain_mlp_row)[0].astype(bf16)

    normed_mlp, group_cotangent = lax.optimization_barrier((normed_mlp, group_cotangent))
    group_normed = lax.all_gather(normed_mlp, PLANE, axis=0, tiled=True)
    w_down_here, w_gate_up_here = w_ff[:, :ff_here], w_ff[:, ff_here:]
    grad_hidden = dot(group_cotangent, w_down_here)
    grad_hidden, group_normed = lax.optimization_barrier((grad_hidden, group_normed))
    gate_up = dot(group_normed, w_gate_up_here)
    gate, up = gate_up[:, :ff_here], gate_up[:, ff_here:]
    sigmoid = jax.nn.sigmoid(gate)
    silu = gate * sigmoid
    hidden = (silu * up).astype(bf16)
    grad_gate = (grad_hidden * up * (sigmoid + silu * (1.0 - sigmoid))).astype(bf16)
    grad_up = (grad_hidden * silu).astype(bf16)
    grad_gate_up = jnp.concatenate([grad_gate, grad_up], axis=1)
    grad_part = dot_cols(grad_gate_up, w_gate_up_here).astype(bf16)
    grad_normed_mlp = lax.psum_scatter(grad_part, PLANE, scatter_dimension=0, tiled=True)
    down_part = dot_rows(group_cotangent, hidden).astype(bf16)
    gate_part = dot_rows(group_normed, grad_gate).astype(bf16)
    up_part = dot_rows(group_normed, grad_up).astype(bf16)

    def over_wide(part):
        parts = part.reshape(wide_count, rows_wide, -1)
        total = lax.dynamic_index_in_dim(parts, wide_at, 0, keepdims=False).astype(f32)
        for d in others:
            theirs = lax.dynamic_index_in_dim(parts, wide_at ^ d, 0, keepdims=False)
            total = total + partner(theirs, WIDE, d).astype(f32)
        return total.astype(bf16)

    sums_ff = [over_wide(part) for part in (down_part, gate_part, up_part)]
    grad_normed_mlp, *sums_ff = lax.optimization_barrier((grad_normed_mlp, *sums_ff))
    ff_all = lax.all_gather(
        jnp.concatenate(
            [total[:, :main] for total in sums_ff] + [total[:, main:] for total in sums_ff],
            axis=1,
        ),
        PLANE,
        axis=0,
    )

    _, scaled_mlp, inverse_mlp = rms_parts(middle, gain_mlp_row)
    grad_middle, grad_gain_mlp = rms_back(
        grad_normed_mlp.astype(f32), scaled_mlp, inverse_mlp, gain_mlp_row
    )
    grad_middle = cotangent.reshape(-1, width).astype(f32) + grad_middle
    grad_branch = grad_middle.astype(bf16).reshape(tokens.shape)
    branch_pair = jnp.stack([grad_branch, partner(grad_branch, "hx")])

    blk_branch = block_major(branch_pair, partner(branch_pair, "core")).reshape(-1, width)
    grad_heads = dot(blk_branch, w_out_head).astype(bf16)
    hidden, grad_heads = lax.optimization_barrier((hidden, grad_heads))
    out_part = dot_cols(hidden, w_down_here).astype(bf16)
    grad_heads = grad_heads.reshape(queries.shape)
    row_inner = jnp.sum(grad_heads.astype(f32) * attention, axis=-1)
    probs = jnp.exp(masked - log_total)
    grad_probs = jnp.einsum(
        "asrhd,kscd->asrhkc", grad_heads, all_values, preferred_element_type=f32
    )
    grad_scores = (probs * (grad_probs - row_inner[..., None, None])).astype(bf16)
    grad_queries = (
        jnp.einsum("asrhkc,kscd->asrhd", grad_scores, all_keys, preferred_element_type=f32) * scale
    )
    grad_queries = turn_back(
        grad_queries.reshape(-1, heads_here, HEAD_SIZE),
        cosine_table[:, None, :],
        sine_values[:, None, :],
    ).reshape(-1, q_here)
    grad_keys = (
        jnp.einsum("asrhkc,asrhd->kscd", grad_scores, queries, preferred_element_type=f32) * scale
    )
    grad_values = jnp.einsum(
        "asrhkc,asrhd->kscd", probs.astype(bf16), grad_heads, preferred_element_type=f32
    )
    kept, given = in_order([grad_keys, grad_values], core_at)
    kept = kept + partner(given.astype(bf16), "core").astype(f32)
    kept = kept.reshape(blk_count, blk_rows, HEAD_SIZE)
    sent_pair = [kept[blk_count - d].astype(bf16) for d in range(1, blk_count)]
    out_grad_part = dot_rows(blk_branch, attended_head)
    grad_pair = kept[0]
    for d in range(1, blk_count):
        grad_pair = grad_pair + shifted(sent_pair[d - 1], "blk", d).astype(f32)
    grad_pair = jnp.where(
        core_at == 0, turn_back(grad_pair, cosine_table, sine_values), grad_pair
    )
    grad_projected = jnp.concatenate([grad_queries, grad_pair], axis=1).astype(bf16)
    w_back = jnp.concatenate(
        [
            w_head[:, :q_here],
            jnp.where(
                core_at == 0,
                w_head[:, q_here : q_here + HEAD_SIZE],
                w_head[:, q_here + HEAD_SIZE :],
            ),
        ],
        axis=1,
    )
    back_part = dot_cols(grad_projected, w_back).astype(bf16)
    back_part = back_part.reshape(slot_count, seq_count, 2, 2, rows_dev, width)
    own_c, other_c = in_order([back_part[:, :, 0], back_part[:, :, 1]], core_at)

    qkv_part = dot_rows(normed_attn, grad_projected)
    proj_part = jnp.concatenate(
        [qkv_part[:, :q_here], out_grad_part, qkv_part[:, q_here:]], axis=1
    ).astype(bf16)
    proj_part = proj_part.reshape(wide_count, rows_wide, -1)
    proj_sum = lax.dynamic_index_in_dim(proj_part, wide_at, 0, keepdims=False).astype(f32)
    for d in others:
        theirs = lax.dynamic_index_in_dim(proj_part, wide_at ^ d, 0, keepdims=False)
        proj_sum = proj_sum + partner(theirs, WIDE, d).astype(f32)

    own_c = own_c.astype(f32) + partner(other_c, "core").astype(f32)
    given_x = own_c[:, :, 1].astype(bf16)
    grad_normed_attn = own_c[:, :, 0] + partner(given_x, "hx").astype(f32)
    proj_parts = proj_sum.reshape(blk_count, rows_wide // blk_count, -1)
    proj_done = lax.dynamic_index_in_dim(proj_parts, blk_at, 0, keepdims=False)
    for d in range(1, blk_count):
        theirs = lax.dynamic_index_in_dim(proj_parts, blk_at ^ d, 0, keepdims=False)
        proj_done = proj_done + partner(theirs.astype(bf16), "blk", d).astype(f32)
    grad_normed_attn = grad_normed_attn.reshape(-1, width)
    scaled_attn, inverse_attn = rms_parts(flat_tokens, gain_attn_row)[1:]
    grad_flat, grad_gain_attn = rms_back(
        grad_normed_attn, scaled_attn, inverse_attn, gain_attn_row
    )
    input_grad = (grad_middle + grad_flat).astype(bf16).reshape(tokens.shape)
    proj_done, ff_all, out_part = lax.optimization_barrier(
        (proj_done.astype(bf16), ff_all, out_part)
    )
    mlp_out = lax.psum_scatter(out_part, PLANE, scatter_dimension=0, tiled=True)
    proj_blk = [proj_done] + [partner(proj_done, "blk", d) for d in range(1, blk_count)]
    proj_rows = jnp.concatenate(in_order(proj_blk, blk_at))
    proj_pair = jnp.stack(in_order([proj_rows, partner(proj_rows, "hx")], x_at))
    proj_all = in_order([proj_pair, partner(proj_pair, "core")], core_at)

    column_sums = jnp.sum(grad_projected.astype(f32), axis=0)
    bias_sum = jnp.zeros((q_total + 2 * kv_total,), f32)
    bias_sum = lax.dynamic_update_slice(bias_sum, column_sums[:q_here], (head_at * q_here,))
    bias_sum = lax.dynamic_update_slice(
        bias_sum,
        column_sums[q_here:],
        (q_total + core_at * kv_total + kv_at * HEAD_SIZE,),
    )
    sums = jnp.concatenate([bias_sum, grad_gain_attn, grad_gain_mlp.reshape(-1)]).reshape(-1, LANES)
    for axis in ("core", "hx", "blk", WIDE):
        step = 1
        while step < lax.axis_size(axis):
            sums = sums + partner(sums, axis, step)
            step *= 2
    sums = sums.reshape(-1)
    bias_at = q_total + 2 * kv_total
    bias_grad = lax.dynamic_slice_in_dim(sums, wide_at * bias_len, bias_len)
    gain_attn_grad = lax.dynamic_slice_in_dim(sums, bias_at + wide_at * rows_wide, rows_wide)
    gain_mlp_grad = lax.dynamic_slice_in_dim(
        sums, bias_at + width + wide_at * rows_wide, rows_wide
    )

    heads = [(x, c) for x in range(x_count) for c in range(core_count)]
    qkv_grad = jnp.concatenate(
        [proj_all[c][x, :, :q_here] for x, c in heads]
        + [proj_all[c][x, :, 2 * q_here :] for c in range(core_count) for x in range(x_count)],
        axis=1,
    ).astype(f32)
    out_grad = jnp.concatenate(
        [proj_all[c][x, :, q_here : 2 * q_here] for x, c in heads], axis=1
    ).astype(f32)

    def assembled(kinds):
        into = jnp.zeros((rows_wide, len(kinds) * ff), f32)
        at = 0
        for kind in kinds:
            pieces = [ff_all[p, :, kind * main : (kind + 1) * main] for p in range(share)]
            first = 3 * main + kind * LANES
            pieces += [ff_all[e * core_count, :, first : first + LANES] for e in range(extra)]
            for piece in pieces:
                into = lax.dynamic_update_slice(into, piece.astype(f32), (0, at))
                at += piece.shape[1]
        return into

    down_grad, gate_up_grad = assembled([0]), assembled([1, 2])
    output = (middle + mlp_out.astype(f32)).astype(bf16).reshape(tokens.shape)
    return (
        output,
        input_grad,
        qkv_grad,
        bias_grad,
        out_grad,
        gate_up_grad,
        down_grad,
        gain_attn_grad,
        gain_mlp_grad,
    )


def solution(mesh):
    wide, blk, head = mesh.devices.shape
    cores = 2
    fine = Mesh(
        mesh.devices.reshape(wide, blk, head // cores, cores), (WIDE, "blk", "hx", "core")
    )
    rows = P("blk", WIDE, ("hx", "core"), None)
    matrix, vector = P(WIDE, None), P(WIDE)
    in_specs = (
        rows,
        P("blk", WIDE, ("hx", "core")),
        P(),
        matrix,
        vector,
        matrix,
        matrix,
        matrix,
        vector,
        vector,
        rows,
    )
    out_specs = (rows, rows, matrix, vector, matrix, matrix, matrix, vector, vector)
    return jax.shard_map(
        on_device, mesh=fine, in_specs=in_specs, out_specs=out_specs, check_vma=False
    )
```

```python
import jax
import jax.numpy as jnp
from jax import lax
from jax.sharding import Mesh, PartitionSpec as P

QUERY_HEADS = 12
KEY_VALUE_HEADS = 2
HEAD_SIZE = 128
LANES = 128

norm_eps = 1e-06
rope_theta = 1000000.0
masked_score = -1e30

WIDE = "wide"
PLANE = ("blk", "hx", "core")
f32, bf16 = jnp.float32, jnp.bfloat16


def rms_parts(values, gain_row):
    inverse = lax.rsqrt(jnp.mean(values * values, axis=-1, keepdims=True) + norm_eps)
    scaled = values * inverse
    return (scaled * gain_row, scaled, inverse)


def rms_back(grad_normed, scaled, inverse, gain_row):
    grad_scaled = grad_normed * gain_row
    mean_term = jnp.mean(grad_scaled * scaled, axis=-1, keepdims=True)
    return (inverse * (grad_scaled - scaled * mean_term), jnp.sum(grad_normed * scaled, axis=0))


def turn_back(values, cosine_table, sine_values):
    half_size = values.shape[-1] // 2
    turned = values * sine_values
    turned = jnp.concatenate([turned[..., half_size:], turned[..., :half_size]], axis=-1)
    return values * cosine_table + turned


def rope_tables(positions):
    frequency = rope_theta ** (-jnp.arange(0, HEAD_SIZE, 2).astype(f32) / HEAD_SIZE)
    angles = positions.astype(f32)[:, None] * frequency[None, :]
    cosine, sine = jnp.cos(angles), jnp.sin(angles)
    return (
        jnp.concatenate([cosine, cosine], axis=-1),
        jnp.concatenate([-sine, sine], axis=-1),
    )


def dot(a, b):
    return jnp.dot(a, b, preferred_element_type=f32)


def dot_rows(a, b):
    return lax.dot_general(a, b, (((0,), (0,)), ((), ())), preferred_element_type=f32)


def dot_cols(a, b):
    return lax.dot_general(a, b, (((1,), (1,)), ((), ())), preferred_element_type=f32)


def partner(values, axis, distance=1):
    count = lax.axis_size(axis)
    return lax.ppermute(values, axis, [(i, i ^ distance) for i in range(count)])


def shifted(values, axis, distance):
    count = lax.axis_size(axis)
    return lax.ppermute(values, axis, [((i + distance) % count, i) for i in range(count)])


def in_order(pieces, index):
    bit = 1
    while bit < len(pieces):
        odd = (index & bit) != 0
        pieces = [jnp.where(odd, pieces[k ^ bit], pieces[k]) for k in range(len(pieces))]
        bit *= 2
    return pieces


def row_places(index, x_at, rows_dev):
    x_rel = (index // rows_dev) % 2
    core = index // (2 * rows_dev)
    x_abs = jnp.where(x_at == 0, x_rel, 1 - x_rel)
    return (2 * x_abs + core) * rows_dev + index % rows_dev


def on_device(
    tokens,
    positions,
    block_order,
    w_qkv,
    qkv_bias,
    w_out,
    w_gate_up,
    w_down,
    gain_attn,
    gain_mlp,
    cotangent,
):
    slot_count, seq_count, rows_dev, width = tokens.shape
    blk_count, x_count, core_count = (lax.axis_size(a) for a in ("blk", "hx", "core"))
    wide_count = lax.axis_size(WIDE)
    wide_at, blk_at, x_at, core_at = (lax.axis_index(a) for a in (WIDE, "blk", "hx", "core"))
    head_at = x_at * core_count + core_at
    head_shards = x_count * core_count
    heads_here = QUERY_HEADS // head_shards
    q_here = heads_here * HEAD_SIZE
    q_total = QUERY_HEADS * HEAD_SIZE
    kv_total = KEY_VALUE_HEADS * HEAD_SIZE
    kv_at = head_at * KEY_VALUE_HEADS // head_shards
    rows_wide = w_qkv.shape[0]
    half = rows_wide // 2
    block_rows = rows_dev * head_shards
    dev_rows = slot_count * seq_count * rows_dev
    blk_rows = dev_rows * head_shards
    ff = w_down.shape[1]
    others = range(1, wide_count)

    def by_wide(own, pieces):
        return jnp.concatenate(in_order([own] + pieces, wide_at), axis=0)

    def block_major(near, far):
        return jnp.moveaxis(jnp.stack(in_order([near, far], core_at)), (0, 1), (2, 3))

    def head_columns(array):
        return jnp.concatenate(
            [
                lax.dynamic_slice_in_dim(array, head_at * q_here, q_here, 1),
                lax.dynamic_slice_in_dim(array, q_total + kv_at * HEAD_SIZE, HEAD_SIZE, 1),
                lax.dynamic_slice_in_dim(
                    array, q_total + kv_total + kv_at * HEAD_SIZE, HEAD_SIZE, 1
                ),
            ],
            axis=1,
        )

    share = blk_count * x_count * core_count
    main = ff // (LANES * share) * LANES
    extra = (ff - share * main) // LANES
    ff_here = main + LANES

    def ff_columns():
        at = blk_at * x_count + x_at
        has = (core_at == 0) & (at < extra)
        columns = []
        for array, first in ((w_down, 0), (w_gate_up, 0), (w_gate_up, ff)):
            more = lax.dynamic_slice_in_dim(array, first + share * main + at * LANES, LANES, 1)
            columns += [
                lax.dynamic_slice_in_dim(
                    array, first + (at * core_count + core_at) * main, main, 1
                ),
                jnp.where(has, more, jnp.zeros_like(more)),
            ]
        return jnp.concatenate(columns, axis=1)

    tokens_x = partner(tokens, "hx")
    positions_x = partner(positions, "hx")
    small = jnp.concatenate([qkv_bias, gain_attn, gain_mlp])[None]
    small = by_wide(small, [partner(small, WIDE, d) for d in others])
    w_head_own = head_columns(w_qkv)
    w_head_far = [partner(w_head_own, WIDE, d) for d in others]
    cot_rows = cotangent.reshape(-1, width)
    group_cotangent = lax.all_gather(cot_rows, PLANE, axis=0, tiled=True)
    w_out_half = lax.dynamic_slice_in_dim(w_out, core_at * half, half, 0)
    w_out_far = [partner(w_out_half, WIDE, d) for d in others]
    bias_len = qkv_bias.shape[0]
    bias_row = small[:, :bias_len].reshape(1, -1).astype(f32)
    gain_attn_row = small[:, bias_len : bias_len + rows_wide].reshape(1, -1).astype(f32)
    gain_mlp_row = small[:, bias_len + rows_wide :].reshape(1, -1).astype(f32)

    tokens_pair = jnp.stack([tokens, tokens_x])
    positions_pair = jnp.stack([positions, positions_x])
    blk_tokens = block_major(tokens_pair, partner(tokens_pair, "core")).reshape(-1, width)
    blk_positions = block_major(positions_pair, partner(positions_pair, "core")).reshape(-1)
    cosine_table, sine_values = rope_tables(blk_positions)
    w_head = by_wide(w_head_own, w_head_far)
    normed_attn = rms_parts(blk_tokens.astype(f32), gain_attn_row)[0].astype(bf16)
    projected = dot(normed_attn, w_head) + head_columns(bias_row)

    def turned(values):
        moved = jnp.concatenate(
            [values[..., HEAD_SIZE // 2 :], values[..., : HEAD_SIZE // 2]], axis=-1
        )
        return (values * cosine_table[:, None] + moved * sine_values[:, None]).astype(bf16)

    queries = turned(projected[:, :q_here].reshape(-1, heads_here, HEAD_SIZE)).reshape(-1, q_here)
    own_keys = turned(projected[:, None, q_here : q_here + HEAD_SIZE])[:, 0]
    own_values = projected[:, q_here + HEAD_SIZE :].astype(bf16)
    pair = [own_keys, own_values]
    sent = jnp.where(core_at == 0, pair[0], pair[1])
    ff_own = ff_columns()
    ff_far = [partner(ff_own, WIDE, d) for d in others]
    arrived = [shifted(sent, "blk", d) for d in range(1, blk_count)]
    arrived = jnp.stack(arrived)
    other = partner(arrived, "core")
    kv_shape = (blk_count * slot_count, seq_count, block_rows, HEAD_SIZE)
    all_keys, all_values = (
        jnp.concatenate([own[None], far]).reshape(kv_shape)
        for own, far in zip(pair, in_order([arrived, other], core_at))
    )
    key_slots = (
        (blk_at + jnp.arange(blk_count, dtype=jnp.int32)) % blk_count * slot_count
    )[:, None] + jnp.arange(slot_count, dtype=jnp.int32)[None]
    key_order = jnp.take(block_order, key_slots.reshape(-1))

    query_order = key_order[:slot_count]
    places = row_places(jnp.arange(block_rows, dtype=jnp.int32), x_at, rows_dev)
    queries = queries.reshape(slot_count, seq_count, block_rows, heads_here, HEAD_SIZE)
    scale = HEAD_SIZE**-0.5
    allowed = (
        places[None, None, None, None, None, :]
        <= places[None, None, :, None, None, None]
        + (query_order[:, None] - key_order[None, :])[:, None, None, None, :, None] * block_rows
    )
    scores = jnp.einsum("asrhd,kscd->asrhkc", queries, all_keys, preferred_element_type=f32)
    masked = jnp.where(allowed, scores * scale, masked_score)
    peak = jnp.max(masked, axis=(-2, -1), keepdims=True)
    weights = jnp.exp(masked - peak)
    total = jnp.sum(weights, axis=(-2, -1), keepdims=True)
    log_total = peak + jnp.log(total)
    attention = jnp.einsum(
        "asrhkc,kscd->asrhd", (weights / total).astype(bf16), all_values, preferred_element_type=f32
    )
    attended_head = attention.astype(bf16).reshape(blk_rows, q_here)
    back = attended_head.reshape(slot_count, seq_count, 2, 2, rows_dev, q_here)
    back_x = back[:, :, :, 1]
    from_x = partner(back_x, "hx")

    out_far = [
        jnp.concatenate(in_order([far, partner(far, "core")], core_at), axis=0)
        for far in w_out_far
    ]
    full_out = by_wide(w_out, out_far)
    w_out_head = lax.dynamic_slice_in_dim(full_out, head_at * q_here, q_here, 1)
    w_ff = by_wide(ff_own, ff_far)

    by_x = jnp.stack([back[:, :, :, 0], from_x])
    own_c, other_c = in_order([by_x[:, :, :, 0], by_x[:, :, :, 1]], core_at)
    by_core = in_order([own_c, partner(other_c, "core")], core_at)
    by_head = [
        piece for x_piece in zip(*(in_order(list(p), x_at) for p in by_core)) for piece in x_piece
    ]
    attended = jnp.concatenate(by_head, axis=-1).reshape(dev_rows, q_total)
    flat_tokens = tokens.reshape(-1, width).astype(f32)
    middle = flat_tokens + dot_cols(attended, full_out)
    normed_mlp = rms_parts(middle, gain_mlp_row)[0].astype(bf16)

    normed_mlp, group_cotangent = lax.optimization_barrier((normed_mlp, group_cotangent))
    group_normed = lax.all_gather(normed_mlp, PLANE, axis=0, tiled=True)
    w_down_here, w_gate_up_here = w_ff[:, :ff_here], w_ff[:, ff_here:]
    grad_hidden = dot(group_cotangent, w_down_here)
    grad_hidden, group_normed = lax.optimization_barrier((grad_hidden, group_normed))
    gate_up = dot(group_normed, w_gate_up_here)
    gate, up = gate_up[:, :ff_here], gate_up[:, ff_here:]
    sigmoid = jax.nn.sigmoid(gate)
    silu = gate * sigmoid
    hidden = (silu * up).astype(bf16)
    grad_gate = (grad_hidden * up * (sigmoid + silu * (1.0 - sigmoid))).astype(bf16)
    grad_up = (grad_hidden * silu).astype(bf16)
    grad_gate_up = jnp.concatenate([grad_gate, grad_up], axis=1)
    grad_part = dot_cols(grad_gate_up, w_gate_up_here).astype(bf16)
    grad_normed_mlp = lax.psum_scatter(grad_part, PLANE, scatter_dimension=0, tiled=True)
    down_part = dot_rows(group_cotangent, hidden).astype(bf16)
    gate_part = dot_rows(group_normed, grad_gate).astype(bf16)
    up_part = dot_rows(group_normed, grad_up).astype(bf16)

    def over_wide(part):
        parts = part.reshape(wide_count, rows_wide, -1)
        total = lax.dynamic_index_in_dim(parts, wide_at, 0, keepdims=False).astype(f32)
        for d in others:
            theirs = lax.dynamic_index_in_dim(parts, wide_at ^ d, 0, keepdims=False)
            total = total + partner(theirs, WIDE, d).astype(f32)
        return total.astype(bf16)

    sums_ff = [over_wide(part) for part in (down_part, gate_part, up_part)]
    left = jnp.concatenate([total[:, main:] for total in sums_ff], axis=1)
    left = left.reshape(core_count, rows_wide // core_count, -1)
    theirs = lax.dynamic_index_in_dim(left, 1 - core_at, 0, keepdims=False)
    left = lax.dynamic_index_in_dim(left, core_at, 0, keepdims=False) + partner(theirs, "core")
    folds = main // LANES
    left = left.reshape(folds, -1, 3 * LANES)
    ff_rows = jnp.concatenate(
        [
            jnp.concatenate([total[:, :main] for total in sums_ff], axis=1),
            jnp.concatenate(list(left), axis=1),
        ]
    )
    grad_normed_mlp, ff_rows = lax.optimization_barrier((grad_normed_mlp, ff_rows))
    ff_all = lax.all_gather(ff_rows, PLANE, axis=0)

    _, scaled_mlp, inverse_mlp = rms_parts(middle, gain_mlp_row)
    grad_middle, grad_gain_mlp = rms_back(
        grad_normed_mlp.astype(f32), scaled_mlp, inverse_mlp, gain_mlp_row
    )
    grad_middle = cotangent.reshape(-1, width).astype(f32) + grad_middle
    grad_branch = grad_middle.astype(bf16).reshape(tokens.shape)
    branch_pair = jnp.stack([grad_branch, partner(grad_branch, "hx")])

    blk_branch = block_major(branch_pair, partner(branch_pair, "core")).reshape(-1, width)
    grad_heads = dot(blk_branch, w_out_head).astype(bf16)
    hidden, grad_heads = lax.optimization_barrier((hidden, grad_heads))
    out_part = dot_cols(hidden, w_down_here).astype(bf16)
    grad_heads = grad_heads.reshape(queries.shape)
    row_inner = jnp.sum(grad_heads.astype(f32) * attention, axis=-1)
    probs = jnp.exp(masked - log_total)
    grad_probs = jnp.einsum(
        "asrhd,kscd->asrhkc", grad_heads, all_values, preferred_element_type=f32
    )
    grad_scores = (probs * (grad_probs - row_inner[..., None, None])).astype(bf16)
    grad_queries = (
        jnp.einsum("asrhkc,kscd->asrhd", grad_scores, all_keys, preferred_element_type=f32) * scale
    )
    grad_queries = turn_back(
        grad_queries.reshape(-1, heads_here, HEAD_SIZE),
        cosine_table[:, None, :],
        sine_values[:, None, :],
    ).reshape(-1, q_here)
    grad_keys = (
        jnp.einsum("asrhkc,asrhd->kscd", grad_scores, queries, preferred_element_type=f32) * scale
    )
    grad_values = jnp.einsum(
        "asrhkc,asrhd->kscd", probs.astype(bf16), grad_heads, preferred_element_type=f32
    )
    kept, given = in_order([grad_keys, grad_values], core_at)
    kept = kept + partner(given.astype(bf16), "core").astype(f32)
    kept = kept.reshape(blk_count, blk_rows, HEAD_SIZE)
    sent_pair = [kept[blk_count - d].astype(bf16) for d in range(1, blk_count)]
    out_grad_part = dot_rows(blk_branch, attended_head)
    grad_pair = kept[0]
    for d in range(1, blk_count):
        grad_pair = grad_pair + shifted(sent_pair[d - 1], "blk", d).astype(f32)
    grad_pair = jnp.where(
        core_at == 0, turn_back(grad_pair, cosine_table, sine_values), grad_pair
    )
    grad_projected = jnp.concatenate([grad_queries, grad_pair], axis=1).astype(bf16)
    w_back = jnp.concatenate(
        [
            w_head[:, :q_here],
            jnp.where(
                core_at == 0,
                w_head[:, q_here : q_here + HEAD_SIZE],
                w_head[:, q_here + HEAD_SIZE :],
            ),
        ],
        axis=1,
    )
    back_part = dot_cols(grad_projected, w_back).astype(bf16)
    back_part = back_part.reshape(slot_count, seq_count, 2, 2, rows_dev, width)
    own_c, other_c = in_order([back_part[:, :, 0], back_part[:, :, 1]], core_at)

    qkv_part = dot_rows(normed_attn, grad_projected)
    proj_part = jnp.concatenate(
        [qkv_part[:, :q_here], out_grad_part, qkv_part[:, q_here:]], axis=1
    ).astype(bf16)
    proj_part = proj_part.reshape(wide_count, rows_wide, -1)
    proj_sum = lax.dynamic_index_in_dim(proj_part, wide_at, 0, keepdims=False).astype(f32)
    for d in others:
        theirs = lax.dynamic_index_in_dim(proj_part, wide_at ^ d, 0, keepdims=False)
        proj_sum = proj_sum + partner(theirs, WIDE, d).astype(f32)

    own_c = own_c.astype(f32) + partner(other_c, "core").astype(f32)
    given_x = own_c[:, :, 1].astype(bf16)
    grad_normed_attn = own_c[:, :, 0] + partner(given_x, "hx").astype(f32)
    proj_parts = proj_sum.reshape(blk_count, rows_wide // blk_count, -1)
    proj_done = lax.dynamic_index_in_dim(proj_parts, blk_at, 0, keepdims=False)
    for d in range(1, blk_count):
        theirs = lax.dynamic_index_in_dim(proj_parts, blk_at ^ d, 0, keepdims=False)
        proj_done = proj_done + partner(theirs.astype(bf16), "blk", d).astype(f32)
    grad_normed_attn = grad_normed_attn.reshape(-1, width)
    scaled_attn, inverse_attn = rms_parts(flat_tokens, gain_attn_row)[1:]
    grad_flat, grad_gain_attn = rms_back(
        grad_normed_attn, scaled_attn, inverse_attn, gain_attn_row
    )
    input_grad = (grad_middle + grad_flat).astype(bf16).reshape(tokens.shape)
    proj_done, ff_all, out_part = lax.optimization_barrier(
        (proj_done.astype(bf16), ff_all, out_part)
    )
    mlp_out = lax.psum_scatter(out_part, PLANE, scatter_dimension=0, tiled=True)
    proj_blk = [proj_done] + [partner(proj_done, "blk", d) for d in range(1, blk_count)]
    proj_rows = jnp.concatenate(in_order(proj_blk, blk_at))
    proj_pair = jnp.stack(in_order([proj_rows, partner(proj_rows, "hx")], x_at))
    proj_all = in_order([proj_pair, partner(proj_pair, "core")], core_at)

    column_sums = jnp.sum(grad_projected.astype(f32), axis=0)
    bias_sum = jnp.zeros((q_total + 2 * kv_total,), f32)
    bias_sum = lax.dynamic_update_slice(bias_sum, column_sums[:q_here], (head_at * q_here,))
    bias_sum = lax.dynamic_update_slice(
        bias_sum,
        column_sums[q_here:],
        (q_total + core_at * kv_total + kv_at * HEAD_SIZE,),
    )
    sums = jnp.concatenate([bias_sum, grad_gain_attn, grad_gain_mlp.reshape(-1)]).reshape(-1, LANES)
    for axis in ("core", "hx", "blk", WIDE):
        step = 1
        while step < lax.axis_size(axis):
            sums = sums + partner(sums, axis, step)
            step *= 2
    sums = sums.reshape(-1)
    bias_at = q_total + 2 * kv_total
    bias_grad = lax.dynamic_slice_in_dim(sums, wide_at * bias_len, bias_len)
    gain_attn_grad = lax.dynamic_slice_in_dim(sums, bias_at + wide_at * rows_wide, rows_wide)
    gain_mlp_grad = lax.dynamic_slice_in_dim(
        sums, bias_at + width + wide_at * rows_wide, rows_wide
    )

    heads = [(x, c) for x in range(x_count) for c in range(core_count)]
    qkv_grad = jnp.concatenate(
        [proj_all[c][x, :, :q_here] for x, c in heads]
        + [proj_all[c][x, :, 2 * q_here :] for c in range(core_count) for x in range(x_count)],
        axis=1,
    ).astype(f32)
    out_grad = jnp.concatenate(
        [proj_all[c][x, :, q_here : 2 * q_here] for x, c in heads], axis=1
    ).astype(f32)

    tiles = ff_all[: extra * core_count, rows_wide:]
    tiles = tiles.reshape(extra, core_count, -1, folds, 3 * LANES).transpose(1, 3, 2, 0, 4)
    tiles = tiles.reshape(rows_wide, extra, 3 * LANES)

    def assembled(kinds):
        into = jnp.zeros((rows_wide, len(kinds) * ff), f32)
        at = 0
        for kind in kinds:
            pieces = [
                ff_all[p, :rows_wide, kind * main : (kind + 1) * main] for p in range(share)
            ]
            pieces.append(tiles[:, :, kind * LANES : (kind + 1) * LANES].reshape(rows_wide, -1))
            for piece in pieces:
                into = lax.dynamic_update_slice(into, piece.astype(f32), (0, at))
                at += piece.shape[1]
        return into

    down_grad, gate_up_grad = assembled([0]), assembled([1, 2])
    output = (middle + mlp_out.astype(f32)).astype(bf16).reshape(tokens.shape)
    return (
        output,
        input_grad,
        qkv_grad,
        bias_grad,
        out_grad,
        gate_up_grad,
        down_grad,
        gain_attn_grad,
        gain_mlp_grad,
    )


def solution(mesh):
    wide, blk, head = mesh.devices.shape
    cores = 2
    fine = Mesh(
        mesh.devices.reshape(wide, blk, head // cores, cores), (WIDE, "blk", "hx", "core")
    )
    rows = P("blk", WIDE, ("hx", "core"), None)
    matrix, vector = P(WIDE, None), P(WIDE)
    in_specs = (
        rows,
        P("blk", WIDE, ("hx", "core")),
        P(),
        matrix,
        vector,
        matrix,
        matrix,
        matrix,
        vector,
        vector,
        rows,
    )
    out_specs = (rows, rows, matrix, vector, matrix, matrix, matrix, vector, vector)
    return jax.shard_map(
        on_device, mesh=fine, in_specs=in_specs, out_specs=out_specs, check_vma=False
    )
```
